128 devices in a mesh: chan: 16 (over y_hi, z, core), win: 8 (over y_lo, x).
Axes of the slice: x: 4, y: 4 (y_hi: 2, y_lo: 2; y = y_hi * 2 + y_lo), z: 4, core: 2. Of those that a mesh axis runs over, the one named last changes fastest.
Arguments:
- traces: bfloat16 [16, 8, 6144, 512], P('win', None, 'chan'), may hold values from -13.5 to 13.5
- channel_mask: int32 [6144], P('chan'), may hold values 0 or 1
- source_blocks: int32 [2, 4], replicated, may hold values from 0 to 767
Outputs:
- correlations: float32 [32, 2, 6144, 128], P('win', None, 'chan')
The draws below stay inside these ranges and needn't reach their ends.
All inputs are finite; a program needn't handle non-finite values. No bound on the sum of `channel_mask` on one device may be relied on, other than what follows from the above.
Results may differ from the reference program's by a relative error of at most 0.0072.
Values may be sent and summed in bfloat16 or wider, within the bound.
No kernel may reach another device: no remote copies, remote signals or barrier semaphores. Data moves between devices by JAX's collectives and lax.ppermute only.
A program may use at most 192 MiB of HBM per device.

```python
import math
import jax
import jax.numpy as jnp
from jax import lax

W_DEV = 2
SEG = 8
NT = 512
NF = 128
F_LO = 8
NLAG = 128
VSB = 8
NSRC = 4
STEPS = 2
CHANNELS = 6144
NWIN = 16
NBLK = 768


def draw_traces(key, part):
    key = jax.random.fold_in(key, 11)
    subkeys = jax.random.split(key, 2)
    shape = (NWIN, SEG, CHANNELS, NT)
    channel_gain = jnp.exp(jax.random.uniform(subkeys[0], (1, 1, CHANNELS, 1), jnp.float32, math.log(0.3), math.log(3.0)))
    background = jnp.clip(jax.random.normal(subkeys[1], shape, jnp.float32), -4.5, 4.5)
    return (channel_gain * background).astype(jnp.bfloat16)


def with_ends(array, key, smallest, high):
    index_at = [jax.random.randint(jax.random.fold_in(key, axis), (), 0, length) for axis, length in enumerate(array.shape)]
    longest = array.shape.index(max(array.shape))
    neighbour = index_at[:longest] + [(index_at[longest] + 1) % array.shape[longest]] + index_at[longest + 1:]
    return array.at[tuple(index_at)].set(smallest).at[tuple(neighbour)].set(high)


def setup_inputs(seed: int = 0) -> dict:
    keys = jax.random.split(jax.random.key(seed), 4)
    traces = draw_traces(jax.random.fold_in(keys[3], 71), 0)
    channel_mask = with_ends((jax.random.randint(keys[1], (CHANNELS,), 0, 16) < 15).astype(jnp.int32), jax.random.fold_in(keys[1], 1), 0, 1)
    source_blocks = with_ends(jax.random.randint(keys[2], (STEPS, NSRC), 0, NBLK), jax.random.fold_in(keys[2], 1), 0, NBLK - 1).astype(jnp.int32)
    return dict(traces=traces, channel_mask=channel_mask, source_blocks=source_blocks)


WATER_LEVEL = 0.05
TINY_ENERGY = 1e-06

def spectrum_table(length, bin_count, first_bin):
    sample_times = jnp.arange(length, dtype=jnp.int32)[:, None]
    bin_numbers = first_bin + jnp.arange(bin_count, dtype=jnp.int32)[None, :]
    angles = (sample_times * bin_numbers % length).astype(jnp.float32) * (2.0 * math.pi / length)
    window_taper = 0.5 - 0.5 * jnp.cos((sample_times.astype(jnp.float32) + 0.5) * (2.0 * math.pi / length))
    return jnp.concatenate([window_taper * jnp.cos(angles), -window_taper * jnp.sin(angles)], axis=1).astype(jnp.bfloat16)

def make_lags(length, bin_count, first_bin, lag_count):
    bin_numbers = (first_bin + jnp.arange(bin_count, dtype=jnp.int32))[:, None]
    shifts = (jnp.arange(lag_count, dtype=jnp.int32) - lag_count // 2)[None, :]
    angles = (bin_numbers * shifts % length).astype(jnp.float32) * (2.0 * math.pi / length)
    return jnp.concatenate([jnp.cos(angles), -jnp.sin(angles)], axis=0).astype(jnp.bfloat16)

def whiten(spectrum, bin_count):
    real_part = spectrum[..., :bin_count]
    imag_part = spectrum[..., bin_count:]
    energy = real_part * real_part + imag_part * imag_part
    mean_energy = lax.optimization_barrier(jnp.mean(energy, axis=-1, keepdims=True))
    factor = lax.rsqrt(energy + WATER_LEVEL * mean_energy + TINY_ENERGY)
    return jnp.concatenate([real_part * factor, imag_part * factor], axis=-1)

def cross_spectra(senders, receivers, bin_count):
    senders = senders.astype(jnp.float32)
    receivers = receivers.astype(jnp.float32)

    def correlate_bins(left, right):
        return jnp.einsum('nif,njf->ifj', left, right, precision=lax.Precision.HIGHEST)
    send_real, send_imag = (senders[..., :bin_count], senders[..., bin_count:])
    recv_real, recv_imag = (receivers[..., :bin_count], receivers[..., bin_count:])
    in_phase = correlate_bins(send_real, recv_real) + correlate_bins(send_imag, recv_imag)
    quadrature = correlate_bins(send_real, recv_imag) - correlate_bins(send_imag, recv_real)
    return jnp.concatenate([in_phase, quadrature], axis=1).astype(jnp.bfloat16)

def reference(traces, channel_mask, source_blocks):
    dft_table = spectrum_table(NT, NF, F_LO).astype(jnp.float32)
    live = channel_mask.astype(jnp.float32)

    def one_window(window_traces):
        spectrum = jnp.dot(window_traces.reshape(-1, NT).astype(jnp.float32), dft_table, precision=lax.Precision.HIGHEST).reshape(SEG, CHANNELS, 2 * NF)
        return whiten(spectrum * live[None, :, None], NF).astype(jnp.bfloat16)
    whitened = lax.map(one_window, traces)
    grouped = whitened.reshape(NWIN // W_DEV, W_DEV * SEG, CHANNELS, 2 * NF)
    lag_weights = make_lags(NT, NF, F_LO, NLAG).astype(jnp.float32)
    factor = 1.0 / (NWIN * SEG)
    results = []
    for step_index in range(STEPS):
        chosen = (source_blocks[step_index][:, None] * VSB + jnp.arange(VSB, dtype=jnp.int32)[None, :]).reshape(-1).astype(jnp.int32)

        def add_group(running, group_white, chosen=chosen):
            senders = jnp.take(group_white, chosen, axis=1)
            stacked = lax.optimization_barrier(cross_spectra(senders, group_white, NF))
            return (running + stacked.astype(jnp.float32), None)
        running, _ = lax.scan(add_group, jnp.zeros((NSRC * VSB, 2 * NF, CHANNELS), jnp.float32), grouped)
        results.append(jnp.einsum('igj,gl->ijl', running, lag_weights, precision=lax.Precision.HIGHEST) * factor)
    return jnp.stack(results, axis=1)
```

```python
import functools
import math

import jax
import jax.numpy as jnp
import ml_dtypes
import numpy as np
from jax import lax
from jax.experimental import pallas as pl
from jax.experimental.pallas import tpu as pltpu
from jax.sharding import PartitionSpec as P

NF = 128
F_LO = 8
NLAG = 128
VSB = 8
NSRC = 4
STEPS = 2
WATER_LEVEL = 0.05
TINY_ENERGY = 1e-06

FB = 16
BF16 = jnp.bfloat16
F32 = jnp.float32


def band_rows():
    row = np.arange(2 * NF)
    return F_LO + (row // 16) * 8 + row % 8, (row // 8) % 2


def dft_rows(length):
    bins, part = band_rows()
    t = np.arange(length)
    angle = (t[None, :] * bins[:, None] % length) * (2.0 * math.pi / length)
    taper = 0.5 - 0.5 * np.cos((t + 0.5) * (2.0 * math.pi / length))
    table = np.where(part[:, None] == 0, np.cos(angle), -np.sin(angle)) * taper[None, :]
    return table.astype(np.float32).astype(ml_dtypes.bfloat16)


def lag_rows(length, scale):
    bins, part = band_rows()
    shift = np.arange(NLAG) - NLAG // 2
    angle = (shift[:, None] * bins[None, :] % length) * (2.0 * math.pi / length)
    table = np.where(part[None, :] == 0, np.cos(angle), -np.sin(angle))
    table = table.astype(np.float32).astype(ml_dtypes.bfloat16)
    return (table.astype(np.float32) * scale).astype(ml_dtypes.bfloat16)


def dot(a, b, dims=((1,), (0,))):
    return lax.dot_general(a, b, (dims, ((), ())), preferred_element_type=F32)


def iota(shape, dim):
    return lax.broadcasted_iota(jnp.int32, shape, dim)


def whiten_rows(z, live=None):
    lanes = z.shape[-1]
    z = z.reshape(FB, 2, 8, lanes)
    re, im = z[:, 0], z[:, 1]
    energy = re * re + im * im
    mean = jnp.sum(jnp.sum(energy, axis=0), axis=0, keepdims=True) * (1.0 / NF)
    factor = lax.rsqrt(energy + WATER_LEVEL * mean[None] + TINY_ENERGY)
    if live is not None:
        factor = factor * live[None]
    out = jnp.concatenate([(re * factor)[:, None], (im * factor)[:, None]], axis=1)
    return out.reshape(FB, 16, lanes).astype(BF16)


def source_kernel(blocks_ref, mask_ref, me_ref, traces_ref, table_ref, *rest):
    keep0, send0, keep1, send1, xbuf, wsc, sems = rest
    count = xbuf.shape[0]
    per_device = traces_ref.shape[1] // VSB
    chan, core = me_ref[0], me_ref[1]
    nblk = STEPS * NSRC
    local, mine, copies = [], [], []
    for b in range(nblk):
        block = blocks_ref[b // NSRC, b % NSRC]
        holder = block // per_device
        loc = block - holder * per_device
        local.append(loc)
        mine.append(holder == chan)
        start = pl.multiple_of((loc // 2) * 16, 16)
        copy = pltpu.make_async_copy(
            traces_ref.at[:, pl.ds(start, 16), :], xbuf.at[:, pl.ds(b * 16, 16), :], sems.at[b]
        )
        copy.start()
        copies.append(copy)
    col = iota((1, 256), 1)
    col_block = (col >> 7) * NSRC + ((col & 31) >> 3)
    col_v = col & 7
    target = jnp.full((1, 256), -100, jnp.int32)
    for b in range(nblk):
        here = col_block == b
        row = jnp.where(mine[b], (local[b] & 1) * 8, -1000)
        target = jnp.where(here, col_v + row, target)
        for v in range(VSB):
            dead = mask_ref[local[b] * VSB + v] == 0
            target = jnp.where(here & (col_v == v) & dead, -1000, target)
    row = iota((512, 256), 0)
    key = ((row >> 7) << 7) + row % 128
    want = jnp.where(target >= 0, (((col >> 5) & 3) << 7) + col_block * 16 + target, -1)
    select = (key == want).astype(F32).astype(BF16)
    for copy in copies:
        copy.wait()

    def one(n, carry):
        z = dot(table_ref[...], xbuf[n], ((1,), (1,)))
        wsc[:, pl.ds(pl.multiple_of(n * 16, 16), 16), :] = whiten_rows(z)
        return carry

    lax.fori_loop(0, count, one, 0, unroll=2)
    for rel, pair in ((0, (keep0, keep1)), (1, (send0, send1))):
        half = core if rel == 0 else 1 - core
        for t in range(2):
            low = half * 2 + t
            left = jnp.concatenate([wsc[hi * 4 + low] for hi in range(4)], axis=1)
            out = dot(left, select).astype(BF16)
            pair[0][t * 256 : (t + 1) * 256, :] = out[:, :128]
            pair[1][t * 256 : (t + 1) * 256, :] = out[:, 128:]


def source_spectra(traces, mask, blocks, me, table):
    count, channels, length = traces.shape
    shape = jax.ShapeDtypeStruct((512, 128), BF16)
    smem = pl.BlockSpec(memory_space=pltpu.SMEM)
    vmem = pl.BlockSpec(memory_space=pltpu.VMEM)
    return pl.pallas_call(
        source_kernel,
        out_shape=[shape] * 4,
        in_specs=[smem, smem, smem, pl.BlockSpec(memory_space=pl.ANY), vmem],
        out_specs=[vmem] * 4,
        scratch_shapes=[
            pltpu.VMEM((count, 128, length), BF16),
            pltpu.VMEM((FB, 256, 128), BF16),
            pltpu.SemaphoreType.DMA((STEPS * NSRC,)),
        ],
        compiler_params=pltpu.CompilerParams(vmem_limit_bytes=32 * 2**20),
        cost_estimate=pl.CostEstimate(flops=10**9, bytes_accessed=3 * 10**6, transcendentals=0),
        name="source_spectra",
    )(blocks, mask, me, traces, table)


def receiver_kernel(traces_ref, table_ref, live_ref, out_ref):
    z = dot(table_ref[...], traces_ref[0], ((1,), (1,)))
    out_ref[:, 0] = whiten_rows(z, live_ref[...])


def receiver_spectra(traces, live, table):
    count, channels, length = traces.shape
    return pl.pallas_call(
        receiver_kernel,
        grid=(count,),
        out_shape=jax.ShapeDtypeStruct((FB, count, 16, channels), BF16),
        in_specs=[
            pl.BlockSpec((1, channels, length), lambda n: (n, 0, 0)),
            pl.BlockSpec((2 * NF, length), lambda n: (0, 0)),
            pl.BlockSpec((1, channels), lambda n: (0, 0)),
        ],
        out_specs=pl.BlockSpec((FB, 1, 16, channels), lambda n: (0, n, 0, 0)),
        compiler_params=pltpu.CompilerParams(vmem_limit_bytes=32 * 2**20),
        cost_estimate=pl.CostEstimate(
            flops=2 * count * channels * length * 256, bytes_accessed=10**7, transcendentals=10**6
        ),
        name="receiver_spectra",
    )(traces, table, live)


def swap_parts(x):
    y = x.astype(F32).reshape(16, 2, 8, x.shape[-1])
    y = jnp.concatenate([-y[:, 1:2], y[:, 0:1]], axis=1)
    return y.reshape(256, x.shape[-1]).astype(BF16)


def correlate_kernel(groups, me_ref, a_ref, b_ref, recv_ref, lag_ref, *rest):
    outs, (pick, both, stacked) = rest[: len(groups)], rest[len(groups) :]
    core, my_y, my_x = me_ref[1], me_ref[2], me_ref[3]
    row, col = iota((512, 256), 0), iota((512, 256), 1)
    rel = row >> 4
    source = (((my_y ^ (rel >> 4)) * 4 + ((my_x + (rel >> 2)) & 3)) << 2) + (rel & 3)
    key = (((row >> 3) & 1) << 7) + source
    for hi in range(4):
        pick[hi] = (col == key + hi * 32).astype(F32).astype(BF16)
    for half, ref in ((0, a_ref), (1, b_ref)):
        for t in range(2):
            x = ref[t * 256 : (t + 1) * 256, :]
            both[half * 2 + t] = jnp.concatenate([x, swap_parts(x)], axis=1)
    diagonal = ((iota((8, 256), 0)) == (iota((8, 256), 1) & 7)).astype(F32)

    def one(u, carry):
        lo, hi = u & 3, u >> 2
        block = hi * 4 + (((lo >> 1) ^ core) << 1) + (lo & 1)
        left = dot(pick[hi], both[lo], ((1,), (1,)))
        left = (left.reshape(64, 8, 256) * diagonal[None]).reshape(512, 256).astype(BF16)
        out = dot(left, recv_ref[block])
        stacked[:, block] = out.astype(BF16).reshape(32, 16, out.shape[-1])
        return carry

    lax.fori_loop(0, 16, one, 0)
    lag = lag_ref[...]
    for group, out in zip(groups, outs):
        for place, (first, amount) in group:

            def two(r, carry, place=place, first=first, out=out):
                x = stacked[first + r].reshape(256, stacked.shape[-1])
                out[place + r] = dot(lag, x).astype(BF16)
                return carry

            lax.fori_loop(0, amount, two, 0)


def correlate(groups, me, a, b, receivers, lags):
    channels = receivers.shape[-1]
    smem = pl.BlockSpec(memory_space=pltpu.SMEM)
    vmem = pl.BlockSpec(memory_space=pltpu.VMEM)
    sizes = [sum(amount for _, (_, amount) in group) for group in groups]
    return pl.pallas_call(
        functools.partial(correlate_kernel, groups),
        out_shape=[jax.ShapeDtypeStruct((n, NLAG, channels), BF16) for n in sizes],
        in_specs=[smem] + [vmem] * 4,
        out_specs=[vmem] * len(groups),
        scratch_shapes=[
            pltpu.VMEM((4, 512, 256), BF16),
            pltpu.VMEM((4, 256, 256), BF16),
            pltpu.VMEM((32, FB, 16, channels), BF16),
        ],
        compiler_params=pltpu.CompilerParams(vmem_limit_bytes=48 * 2**20),
        cost_estimate=pl.CostEstimate(flops=8 * 10**9, bytes_accessed=10**7, transcendentals=0),
        name="correlate",
    )(me, a, b, receivers, lags)


def finish_kernel(*refs):
    ins, out = refs[:-1], refs[-1]
    half = len(ins) // 2
    for step in range(2):
        total = ins[step * half][0].astype(F32)
        for ref in ins[step * half + 1 : (step + 1) * half]:
            total = total + ref[0].astype(F32)
        out[0, step] = total.T


def finish(first, second):
    rows, lags, channels = 4, NLAG, first[0].shape[-1]
    ins = list(first) + list(second)
    spec = pl.BlockSpec((1, lags, channels), lambda r: (r, 0, 0))
    return pl.pallas_call(
        finish_kernel,
        grid=(rows,),
        out_shape=jax.ShapeDtypeStruct((rows, 2, channels, lags), F32),
        in_specs=[spec] * len(ins),
        out_specs=pl.BlockSpec((1, 2, channels, lags), lambda r: (r, 0, 0, 0)),
        compiler_params=pltpu.CompilerParams(vmem_limit_bytes=32 * 2**20),
        name="finish",
    )(*ins)


def add(*xs):
    total = xs[0].astype(F32)
    for x in xs[1:]:
        total = total + x.astype(F32)
    return total.astype(BF16)


def on_device(axes, traces, channel_mask, source_blocks):
    windows, segments, channels, length = traces.shape
    traces = traces.reshape(windows * segments, channels, length)
    chan, win = lax.axis_index("chan"), lax.axis_index("win")
    me = jnp.stack([chan, chan & 1, win >> 2, win & 3]).astype(jnp.int32)
    table = jnp.asarray(dft_rows(length))
    scale = 1.0 / (windows * lax.axis_size("win") * segments)
    lags = jnp.asarray(lag_rows(length, scale))

    def chan_swap(x, bits):
        return lax.ppermute(x, "chan", [(i, i ^ bits) for i in range(16)])

    def win_to(x, dy, dx):
        return lax.ppermute(
            x, "win", [(y * 4 + i, (y ^ dy) * 4 + (i + dx) % 4) for y in range(2) for i in range(4)]
        )

    keep0, send0, keep1, send1 = source_spectra(traces, channel_mask, source_blocks, me, table)

    def share(keep, send):
        mine = keep + chan_swap(send, 1)
        for bits in (2, 6, 8):
            mine = mine + chan_swap(mine, bits)
        return mine, chan_swap(mine, 1)

    live = channel_mask.astype(F32)[None]
    receivers = receiver_spectra(traces, live, table).reshape(FB, 256, channels)

    a, b = share(keep0, send0)
    groups = [((0, (16, 16)),)] + [((0, (dx * 4, 4)),) for dx in range(4)]
    away, o0, o1, o2, o3 = correlate(groups, me, a, b, receivers, lags)
    got = win_to(away, 1, 0)
    up = win_to(add(o2[:2], got[8:10]), 0, 1)
    down = win_to(add(o2[2:], got[10:12]), 0, -1)
    right = jnp.concatenate([add(o1[:2], got[4:6], up), add(o1[2:], got[6:8])])
    left = jnp.concatenate([add(o3[:2], got[12:14]), add(o3[2:], got[14:16], down)])
    first = (o0, got, win_to(right, 0, 1), win_to(left, 0, -1))

    a, b = share(keep1, send1)
    groups = [
        ((0, (0, 4)), (4, (16, 4))),
        ((0, (4, 4)), (4, (20, 4))),
        ((0, (8, 4)),),
        ((0, (24, 4)),),
        ((0, (12, 4)), (4, (28, 4))),
    ]
    x0, x1, x2a, x2b, x3 = correlate(groups, me, a, b, receivers, lags)
    up = win_to(x2a, 0, 1)
    down = win_to(x2b, 0, -1)
    from_left = win_to(jnp.concatenate([add(x1[:4], up), x1[4:]]), 0, 1)
    from_right = win_to(jnp.concatenate([x3[:4], add(x3[4:], down)]), 0, -1)
    got = win_to(add(x0[4:], from_left[4:], from_right[4:]), 1, 0)
    second = (x0, from_left, from_right, got)
    return finish(first, second)


def solution(mesh):
    in_specs = (P("win", None, "chan", None), P("chan"), P())
    out_specs = P("win", None, "chan", None)
    return jax.shard_map(
        functools.partial(on_device, dict(mesh.shape)),
        mesh=mesh,
        in_specs=in_specs,
        out_specs=out_specs,
        check_vma=False,
    )
```

```python
import functools
import math

import jax
import jax.numpy as jnp
import ml_dtypes
import numpy as np
from jax import lax
from jax.experimental import pallas as pl
from jax.experimental.pallas import tpu as pltpu
from jax.sharding import PartitionSpec as P

NF = 128
F_LO = 8
NLAG = 128
VSB = 8
NSRC = 4
STEPS = 2
WATER_LEVEL = 0.05
TINY_ENERGY = 1e-06

FB = 16
BF16 = jnp.bfloat16
F32 = jnp.float32


def band_rows():
    row = np.arange(2 * NF)
    return F_LO + (row // 16) * 8 + row % 8, (row // 8) % 2


def dft_rows(length):
    bins, part = band_rows()
    t = np.arange(length)
    angle = (t[None, :] * bins[:, None] % length) * (2.0 * math.pi / length)
    taper = 0.5 - 0.5 * np.cos((t + 0.5) * (2.0 * math.pi / length))
    table = np.where(part[:, None] == 0, np.cos(angle), -np.sin(angle)) * taper[None, :]
    return table.astype(np.float32).astype(ml_dtypes.bfloat16)


def lag_rows(length, scale):
    bins, part = band_rows()
    shift = np.arange(NLAG) - NLAG // 2
    angle = (shift[:, None] * bins[None, :] % length) * (2.0 * math.pi / length)
    table = np.where(part[None, :] == 0, np.cos(angle), -np.sin(angle))
    table = table.astype(np.float32).astype(ml_dtypes.bfloat16)
    return (table.astype(np.float32) * scale).astype(ml_dtypes.bfloat16)


def dot(a, b, dims=((1,), (0,))):
    return lax.dot_general(a, b, (dims, ((), ())), preferred_element_type=F32)


def iota(shape, dim):
    return lax.broadcasted_iota(jnp.int32, shape, dim)


def whiten_rows(z, live=None):
    lanes = z.shape[-1]
    z = z.reshape(FB, 2, 8, lanes)
    re, im = z[:, 0], z[:, 1]
    energy = re * re + im * im
    mean = jnp.sum(jnp.sum(energy, axis=0), axis=0, keepdims=True) * (1.0 / NF)
    factor = lax.rsqrt(energy + WATER_LEVEL * mean[None] + TINY_ENERGY)
    if live is not None:
        factor = factor * live[None]
    out = jnp.concatenate([(re * factor)[:, None], (im * factor)[:, None]], axis=1)
    return out.reshape(FB, 16, lanes).astype(BF16)


def source_kernel(blocks_ref, mask_ref, me_ref, traces_ref, table_ref, *rest):
    keep0, send0, keep1, send1, xbuf, wsc, sems = rest
    count = xbuf.shape[0]
    per_device = traces_ref.shape[1] // VSB
    chan, core = me_ref[0], me_ref[1]
    nblk = STEPS * NSRC
    local, mine, copies = [], [], []
    for b in range(nblk):
        block = blocks_ref[b // NSRC, b % NSRC]
        holder = block // per_device
        loc = block - holder * per_device
        local.append(loc)
        mine.append(holder == chan)
        start = pl.multiple_of((loc // 2) * 16, 16)
        copy = pltpu.make_async_copy(
            traces_ref.at[:, pl.ds(start, 16), :], xbuf.at[:, pl.ds(b * 16, 16), :], sems.at[b]
        )
        copy.start()
        copies.append(copy)
    col = iota((1, 256), 1)
    col_block = (col >> 7) * NSRC + ((col & 31) >> 3)
    col_v = col & 7
    target = jnp.full((1, 256), -100, jnp.int32)
    for b in range(nblk):
        here = col_block == b
        row = jnp.where(mine[b], (local[b] & 1) * 8, -1000)
        target = jnp.where(here, col_v + row, target)
        for v in range(VSB):
            dead = mask_ref[local[b] * VSB + v] == 0
            target = jnp.where(here & (col_v == v) & dead, -1000, target)
    row = iota((512, 256), 0)
    key = ((row >> 7) << 7) + row % 128
    want = jnp.where(target >= 0, (((col >> 5) & 3) << 7) + col_block * 16 + target, -1)
    select = (key == want).astype(F32).astype(BF16)
    for copy in copies:
        copy.wait()

    def one(n, carry):
        z = dot(table_ref[...], xbuf[n], ((1,), (1,)))
        wsc[:, pl.ds(pl.multiple_of(n * 16, 16), 16), :] = whiten_rows(z)
        return carry

    lax.fori_loop(0, count, one, 0, unroll=16)
    for rel, pair in ((0, (keep0, keep1)), (1, (send0, send1))):
        half = core if rel == 0 else 1 - core
        for t in range(2):
            low = half * 2 + t
            left = jnp.concatenate([wsc[hi * 4 + low] for hi in range(4)], axis=1)
            out = dot(left, select).astype(BF16)
            pair[0][t * 256 : (t + 1) * 256, :] = out[:, :128]
            pair[1][t * 256 : (t + 1) * 256, :] = out[:, 128:]


def source_spectra(traces, mask, blocks, me, table):
    count, channels, length = traces.shape
    shape = jax.ShapeDtypeStruct((512, 128), BF16)
    smem = pl.BlockSpec(memory_space=pltpu.SMEM)
    vmem = pl.BlockSpec(memory_space=pltpu.VMEM)
    return pl.pallas_call(
        source_kernel,
        out_shape=[shape] * 4,
        in_specs=[smem, smem, smem, pl.BlockSpec(memory_space=pl.ANY), vmem],
        out_specs=[vmem] * 4,
        scratch_shapes=[
            pltpu.VMEM((count, 128, length), BF16),
            pltpu.VMEM((FB, 256, 128), BF16),
            pltpu.SemaphoreType.DMA((STEPS * NSRC,)),
        ],
        compiler_params=pltpu.CompilerParams(vmem_limit_bytes=60 * 2**20),
        cost_estimate=pl.CostEstimate(flops=10**9, bytes_accessed=3 * 10**6, transcendentals=0),
        name="source_spectra",
    )(blocks, mask, me, traces, table)


def receiver_kernel(traces_ref, table_ref, live_ref, out_ref):
    for n in range(traces_ref.shape[0]):
        z = dot(table_ref[...], traces_ref[n], ((1,), (1,)))
        out_ref[:, n] = whiten_rows(z, live_ref[...])


def receiver_spectra(traces, live, table):
    count, channels, length = traces.shape
    chunk = math.gcd(count, 4)
    return pl.pallas_call(
        receiver_kernel,
        grid=(count // chunk,),
        out_shape=jax.ShapeDtypeStruct((FB, count, 16, channels), BF16),
        in_specs=[
            pl.BlockSpec((chunk, channels, length), lambda n: (n, 0, 0)),
            pl.BlockSpec((2 * NF, length), lambda n: (0, 0)),
            pl.BlockSpec((1, channels), lambda n: (0, 0)),
        ],
        out_specs=pl.BlockSpec((FB, chunk, 16, channels), lambda n: (0, n, 0, 0)),
        compiler_params=pltpu.CompilerParams(vmem_limit_bytes=32 * 2**20),
        cost_estimate=pl.CostEstimate(
            flops=2 * count * channels * length * 256, bytes_accessed=10**7, transcendentals=10**6
        ),
        name="receiver_spectra",
    )(traces, table, live)


def swap_parts(x):
    y = x.astype(F32).reshape(16, 2, 8, x.shape[-1])
    y = jnp.concatenate([-y[:, 1:2], y[:, 0:1]], axis=1)
    return y.reshape(256, x.shape[-1]).astype(BF16)


def correlate_kernel(groups, me_ref, a_ref, b_ref, recv_ref, lag_ref, *rest):
    outs, (pick, both, stacked) = rest[: len(groups)], rest[len(groups) :]
    core, my_y, my_x = me_ref[1], me_ref[2], me_ref[3]
    row, col = iota((512, 256), 0), iota((512, 256), 1)
    rel = row >> 4
    source = (((my_y ^ (rel >> 4)) * 4 + ((my_x + (rel >> 2)) & 3)) << 2) + (rel & 3)
    key = (((row >> 3) & 1) << 7) + source
    for hi in range(4):
        pick[hi] = (col == key + hi * 32).astype(F32).astype(BF16)
    for half, ref in ((0, a_ref), (1, b_ref)):
        for t in range(2):
            x = ref[t * 256 : (t + 1) * 256, :]
            both[half * 2 + t] = jnp.concatenate([x, swap_parts(x)], axis=1)
    diagonal = ((iota((16, 256), 0) & 7) == (iota((16, 256), 1) & 7)).astype(F32).astype(BF16)

    def one(u, carry):
        lo, hi = u & 3, u >> 2
        block = hi * 4 + (((lo >> 1) ^ core) << 1) + (lo & 1)
        left = dot(pick[hi], both[lo], ((1,), (1,)))
        left = (left.astype(BF16).reshape(32, 16, 256) * diagonal[None]).reshape(512, 256)
        out = dot(left, recv_ref[block])
        stacked[:, block] = out.astype(BF16).reshape(32, 16, out.shape[-1])
        return carry

    lax.fori_loop(0, 16, one, 0, unroll=16)
    lag = lag_ref[...]
    for group, out in zip(groups, outs):
        for place, (first, amount) in group:

            def two(r, carry, place=place, first=first, out=out):
                x = stacked[first + r].reshape(256, stacked.shape[-1])
                out[place + r] = dot(lag, x).astype(BF16)
                return carry

            lax.fori_loop(0, amount, two, 0, unroll=4)


def correlate(groups, me, a, b, receivers, lags):
    channels = receivers.shape[-1]
    smem = pl.BlockSpec(memory_space=pltpu.SMEM)
    vmem = pl.BlockSpec(memory_space=pltpu.VMEM)
    sizes = [sum(amount for _, (_, amount) in group) for group in groups]
    return pl.pallas_call(
        functools.partial(correlate_kernel, groups),
        out_shape=[jax.ShapeDtypeStruct((n, NLAG, channels), BF16) for n in sizes],
        in_specs=[smem] + [vmem] * 4,
        out_specs=[vmem] * len(groups),
        scratch_shapes=[
            pltpu.VMEM((4, 512, 256), BF16),
            pltpu.VMEM((4, 256, 256), BF16),
            pltpu.VMEM((32, FB, 16, channels), BF16),
        ],
        compiler_params=pltpu.CompilerParams(vmem_limit_bytes=48 * 2**20),
        cost_estimate=pl.CostEstimate(flops=8 * 10**9, bytes_accessed=10**7, transcendentals=0),
        name="correlate",
    )(me, a, b, receivers, lags)


def finish_kernel(*refs):
    ins, out = refs[:-1], refs[-1]
    half = len(ins) // 2
    for step in range(2):
        total = ins[step * half][0].astype(F32)
        for ref in ins[step * half + 1 : (step + 1) * half]:
            total = total + ref[0].astype(F32)
        out[0, step] = total.T


def finish(first, second):
    rows, lags, channels = 4, NLAG, first[0].shape[-1]
    ins = list(first) + list(second)
    spec = pl.BlockSpec((1, lags, channels), lambda r: (r, 0, 0))
    return pl.pallas_call(
        finish_kernel,
        grid=(rows,),
        out_shape=jax.ShapeDtypeStruct((rows, 2, channels, lags), F32),
        in_specs=[spec] * len(ins),
        out_specs=pl.BlockSpec((1, 2, channels, lags), lambda r: (r, 0, 0, 0)),
        compiler_params=pltpu.CompilerParams(vmem_limit_bytes=32 * 2**20),
        name="finish",
    )(*ins)


def add(*xs):
    total = xs[0].astype(F32)
    for x in xs[1:]:
        total = total + x.astype(F32)
    return total.astype(BF16)


def on_device(axes, traces, channel_mask, source_blocks):
    windows, segments, channels, length = traces.shape
    traces = traces.reshape(windows * segments, channels, length)
    chan, win = lax.axis_index("chan"), lax.axis_index("win")
    me = jnp.stack([chan, chan & 1, win >> 2, win & 3]).astype(jnp.int32)
    table = jnp.asarray(dft_rows(length))
    scale = 1.0 / (windows * lax.axis_size("win") * segments)
    lags = jnp.asarray(lag_rows(length, scale))

    def chan_swap(x, bits):
        return lax.ppermute(x, "chan", [(i, i ^ bits) for i in range(16)])

    def win_to(x, dy, dx):
        return lax.ppermute(
            x, "win", [(y * 4 + i, (y ^ dy) * 4 + (i + dx) % 4) for y in range(2) for i in range(4)]
        )

    keep0, send0, keep1, send1 = source_spectra(traces, channel_mask, source_blocks, me, table)

    live = channel_mask.astype(F32)[None]
    receivers = receiver_spectra(traces, live, table).reshape(FB, 256, channels)

    def share(keep, send, beside):
        mine = keep + chan_swap(send, 1)
        mine = mine + chan_swap(mine, 2)
        mine, beside = lax.optimization_barrier((mine, beside))
        for bits in (6, 8):
            mine = mine + chan_swap(mine, bits)
        return mine, chan_swap(mine, 1), beside

    a, b, receivers = share(keep0, send0, receivers)
    groups = [((0, (16, 16)),)] + [((0, (dx * 4, 4)),) for dx in range(4)]
    away, o0, o1, o2, o3 = correlate(groups, me, a, b, receivers, lags)
    share1 = share(keep1, send1, receivers)
    a, b, receivers, away = lax.optimization_barrier((*share1, away))
    got = win_to(away, 1, 0)
    up = win_to(add(o2[:2], got[8:10]), 0, 1)
    down = win_to(add(o2[2:], got[10:12]), 0, -1)
    right = jnp.concatenate([add(o1[:2], got[4:6], up), add(o1[2:], got[6:8])])
    left = jnp.concatenate([add(o3[:2], got[12:14]), add(o3[2:], got[14:16], down)])
    first = (o0, got, win_to(right, 0, 1), win_to(left, 0, -1))

    groups = [
        ((0, (0, 4)), (4, (16, 4))),
        ((0, (4, 4)), (4, (20, 4))),
        ((0, (8, 4)),),
        ((0, (24, 4)),),
        ((0, (12, 4)), (4, (28, 4))),
    ]
    x0, x1, x2a, x2b, x3 = correlate(groups, me, a, b, receivers, lags)
    up = win_to(x2a, 0, 1)
    down = win_to(x2b, 0, -1)
    from_left = win_to(jnp.concatenate([add(x1[:4], up), x1[4:]]), 0, 1)
    from_right = win_to(jnp.concatenate([x3[:4], add(x3[4:], down)]), 0, -1)
    got = win_to(add(x0[4:], from_left[4:], from_right[4:]), 1, 0)
    second = (x0, from_left, from_right, got)
    return finish(first, second)


def solution(mesh):
    in_specs = (P("win", None, "chan", None), P("chan"), P())
    out_specs = P("win", None, "chan", None)
    return jax.shard_map(
        functools.partial(on_device, dict(mesh.shape)),
        mesh=mesh,
        in_specs=in_specs,
        out_specs=out_specs,
        check_vma=False,
    )
```

```python
import functools
import math

import jax
import jax.numpy as jnp
import ml_dtypes
import numpy as np
from jax import lax
from jax.experimental import pallas as pl
from jax.experimental.pallas import tpu as pltpu
from jax.sharding import PartitionSpec as P

NF = 128
F_LO = 8
NLAG = 128
VSB = 8
NSRC = 4
STEPS = 2
WATER_LEVEL = 0.05
TINY_ENERGY = 1e-06

FB = 16
BF16 = jnp.bfloat16
F32 = jnp.float32
MB = 2**20

PLACES = ((0, 0), (0, 1), (0, 2), (0, 3), (1, 0), (1, 1), (1, 3))
KEPT = (((0, 0), (0, 1), (0, 2), (0, 3)), ((0, 0), (0, 3), (1, 0), (1, 3)), ((0, 0), (0, 1), (1, 0), (1, 1)))
PAIRS = ((1, 0), (0, 1), (0, 3))
PARTS_12 = (
    ((1, (1, 0), 0, 2), (1, (1, 3), 0, 2), (2, (1, 0), 0, 2), (2, (1, 1), 0, 2)),
    ((2, (0, 1), 2, 2), (2, (1, 1), 2, 2)),
    ((1, (0, 3), 2, 2), (1, (1, 3), 2, 2)),
    ((1, (0, 0), 0, 4),),
    ((1, (0, 3), 0, 2),),
    ((1, (1, 0), 2, 2),),
    ((2, (0, 0), 0, 4),),
    ((2, (0, 1), 0, 2),),
    ((2, (1, 0), 2, 2),),
)
PARTS_0 = (
    ((0, (0, 2), 0, 2),),
    ((0, (0, 2), 2, 2),),
    ((0, (0, 0), 0, 4),),
    ((0, (0, 1), 0, 4),),
    ((0, (0, 3), 0, 4),),
)


def band_rows():
    row = np.arange(2 * NF)
    return F_LO + (row // 16) * 8 + row % 8, (row // 8) % 2


def dft_rows(length):
    bins, part = band_rows()
    t = np.arange(length)
    angle = (t[None, :] * bins[:, None] % length) * (2.0 * math.pi / length)
    taper = 0.5 - 0.5 * np.cos((t + 0.5) * (2.0 * math.pi / length))
    table = np.where(part[:, None] == 0, np.cos(angle), -np.sin(angle)) * taper[None, :]
    return table.astype(np.float32).astype(ml_dtypes.bfloat16)


def lag_rows(length, scale):
    bins, part = band_rows()
    shift = np.arange(NLAG) - NLAG // 2
    angle = (shift[:, None] * bins[None, :] % length) * (2.0 * math.pi / length)
    table = np.where(part[None, :] == 0, np.cos(angle), -np.sin(angle))
    table = table.astype(np.float32).astype(ml_dtypes.bfloat16)
    return (table.astype(np.float32) * scale).astype(ml_dtypes.bfloat16)


def dot(a, b, dims=((1,), (0,))):
    return lax.dot_general(a, b, (dims, ((), ())), preferred_element_type=F32)


def iota(shape, dim):
    return lax.broadcasted_iota(jnp.int32, shape, dim)


def whiten_rows(z, live):
    lanes = z.shape[-1]
    z = z.reshape(FB, 2, 8, lanes)
    re, im = z[:, 0], z[:, 1]
    energy = re * re + im * im
    mean = jnp.sum(jnp.sum(energy, axis=0), axis=0, keepdims=True) * (1.0 / NF)
    factor = lax.rsqrt(energy + WATER_LEVEL * mean[None] + TINY_ENERGY) * live[None]
    out = jnp.concatenate([(re * factor)[:, None], (im * factor)[:, None]], axis=1)
    return out.reshape(FB, 16, lanes).astype(BF16)


def spectra_kernel(blocks_ref, traces_ref, table_ref, mask_ref, *rest):
    thirds, (keep0, keep1, send0, send1) = rest[:3], rest[3:]
    chunk, channels = traces_ref.shape[0], traces_ref.shape[1]
    step = pl.program_id(0)
    live = mask_ref[...].astype(F32)[None]
    for n in range(chunk):
        z = dot(table_ref[...], traces_ref[n], ((1,), (1,)))
        w = whiten_rows(z, live)
        start = pl.multiple_of((step * chunk + n) * 16, 16)
        for third, ref in enumerate(thirds):
            ref[:, pl.ds(start, 16), :] = w[:, :, third * 128 : (third + 1) * 128]

    @pl.when(step == pl.num_programs(0) - 1)
    def _():
        chan = lax.axis_index("chan")
        core = chan & 1
        per_device = channels // VSB
        col = iota((1, 256), 1)
        col_block = (col >> 7) * NSRC + ((col & 31) >> 3)
        want = jnp.full((1, 256), -1, jnp.int32)
        for b in range(STEPS * NSRC):
            block = blocks_ref[b // NSRC, b % NSRC]
            holder = block // per_device
            first = jnp.where(holder == chan, (block - holder * per_device) * VSB, -1000)
            want = jnp.where(col_block == b, first + (col & 7), want)
        row = iota((channels, 256), 0)
        select = [
            (row == jnp.where(((col >> 5) & 3) == hi, want, -1)).astype(F32).astype(BF16)
            for hi in range(4)
        ]
        select = jnp.concatenate(select, axis=0)
        for half, pair in ((core, (keep0, keep1)), (1 - core, (send0, send1))):
            for t in range(2):
                low = half * 2 + t
                left = jnp.concatenate(
                    [ref[hi * 4 + low] for hi in range(4) for ref in thirds], axis=1
                )
                out = dot(left, select).astype(BF16)
                pair[0][t * 256 : (t + 1) * 256, :] = out[:, :128]
                pair[1][t * 256 : (t + 1) * 256, :] = out[:, 128:]


def spectra(traces, mask, blocks, table):
    count, channels, length = traces.shape
    chunk = math.gcd(count, 4)
    smem = pl.BlockSpec(memory_space=pltpu.SMEM)
    third = jax.ShapeDtypeStruct((FB, count * 16, channels // 3), BF16)
    shape = jax.ShapeDtypeStruct((512, 128), BF16)
    return pl.pallas_call(
        spectra_kernel,
        grid=(count // chunk,),
        out_shape=[third] * 3 + [shape] * 4,
        in_specs=[
            smem,
            pl.BlockSpec((chunk, channels, length), lambda n: (n, 0, 0)),
            pl.BlockSpec((2 * NF, length), lambda n: (0, 0)),
            pl.BlockSpec((channels,), lambda n: (0,)),
        ],
        out_specs=[pl.BlockSpec(third.shape, lambda n: (0, 0, 0))] * 3
        + [pl.BlockSpec((512, 128), lambda n: (0, 0))] * 4,
        compiler_params=pltpu.CompilerParams(vmem_limit_bytes=60 * MB),
        cost_estimate=pl.CostEstimate(flops=10**9, bytes_accessed=10**7, transcendentals=0),
        name="spectra",
    )(blocks, traces, table, mask)


def swap_parts(x):
    y = x.astype(F32).reshape(16, 2, 8, x.shape[-1])
    y = jnp.concatenate([-y[:, 1:2], y[:, 0:1]], axis=1)
    return y.reshape(256, x.shape[-1]).astype(BF16)


def pick_kernel(pick):
    win = lax.axis_index("win")
    my_y, my_x = win >> 2, win & 3
    for g, (ey, ex) in enumerate(PLACES):
        row, col = iota((64, 256), 0), iota((64, 256), 1)
        source = ((((my_y ^ ey) * 4) + (my_x ^ ex)) << 2) + (row >> 4)
        key = (((row >> 3) & 1) << 7) + source
        for hi in range(4):
            pick[hi, g * 64 : (g + 1) * 64, :] = (col == key + hi * 32).astype(F32).astype(BF16)


def pick_rows():
    return pl.pallas_call(
        pick_kernel,
        out_shape=jax.ShapeDtypeStruct((4, 64 * len(PLACES), 256), BF16),
        out_specs=pl.BlockSpec(memory_space=pltpu.VMEM),
        cost_estimate=pl.CostEstimate(flops=10**6, bytes_accessed=10**6, transcendentals=0),
        name="pick_rows",
    )()


def correlate_kernel(thirds, steps, parts, *rest):
    nt = len(thirds)
    rest = list(rest)
    ins = [rest.pop(0) for _ in range(4 + 4 * nt)]
    outs = [rest.pop(0) for _ in parts]
    results = [rest.pop(0) for _ in parts]
    pick, lag_ref, senders, held, both, stacked, sems, out_sems = rest
    core = lax.axis_index("chan") & 1
    targets = [pick, lag_ref] + [senders.at[i] for i in range(2 + 2 * nt)]
    early = [
        pltpu.make_async_copy(src, dst, sems.at[i])
        for i, (src, dst) in enumerate(zip(ins, targets))
    ]
    sources = ins[len(early) :]
    late = [
        [
            pltpu.make_async_copy(
                ref.at[pl.ds(hi * 4, 4)],
                held.at[i, pl.ds(hi * 4, 4)],
                sems.at[len(early) + hi * 2 * nt + i],
            )
            for i, ref in enumerate(sources)
        ]
        for hi in range(4)
    ]
    for copy in early[2:] + early[:2]:
        copy.start()
    for some in late:
        for copy in some:
            copy.start()
    diagonal = ((iota((16, 256), 0) & 7) == (iota((16, 256), 1) & 7)).astype(F32).astype(BF16)
    rows_of = sorted({place for t in thirds for place in KEPT[t]})

    def spread(rows, right):
        left = dot(rows, right, ((1,), (1,))).astype(BF16)
        return (left.reshape(-1, 16, 256) * diagonal[None]).reshape(left.shape)

    def some(x, order, third):
        at = [order.index(place) * 64 for place in KEPT[third]]
        return jnp.concatenate([x[i : i + 64] for i in at], axis=0)

    for who in range(1 + nt):
        for half in range(2):
            early[2 + who * 2 + half].wait()
            for s in range(steps):
                for t in range(2):
                    at = s * 512 + t * 256
                    x = senders[who * 2 + half, at : at + 256, :]
                    both[s, who, half * 2 + t] = jnp.concatenate([x, swap_parts(x)], axis=1)
    early[0].wait()
    for hi in range(4):
        for copy in late[hi]:
            copy.wait()
        rows = pick[hi]
        mine = jnp.concatenate(
            [rows[PLACES.index(p) * 64 : PLACES.index(p) * 64 + 64] for p in rows_of], axis=0
        )
        for lo in range(4):
            block = hi * 4 + (((lo >> 1) ^ core) << 1) + (lo & 1)
            own = [spread(mine, both[s, 0, lo]) for s in range(steps)]
            for i, third in enumerate(thirds):
                left = []
                for s in range(steps):
                    other = spread(some(rows, PLACES, third), both[s, 1 + i, lo])
                    left.append(jnp.concatenate([some(own[s], rows_of, third), other], axis=1))
                left = jnp.concatenate(left, axis=0)
                right = jnp.concatenate([held[i, block], held[nt + i, block]], axis=0)
                out = dot(left, right).astype(BF16).reshape(steps, 16, 16, 128)
                for s in range(steps):
                    stacked[s, i, :, block] = out[s]
    early[1].wait()
    lag = lag_ref[...]
    writes = []
    for p, (part, result, out) in enumerate(zip(parts, results, outs)):
        for s in range(steps):
            place = s * (out.shape[0] // steps)
            for third, where, first, amount in part:
                i, at = thirds.index(third), KEPT[third].index(where) * 4 + first
                for r in range(0, amount, 2):
                    x = [stacked[s, i, at + r + k].reshape(256, 128) for k in range(2)]
                    y = dot(lag, jnp.concatenate(x, axis=1)).astype(BF16)
                    result[place + r], result[place + r + 1] = y[:, :128], y[:, 128:]
                place += amount
        write = pltpu.make_async_copy(result, out, out_sems.at[p])
        write.start()
        writes.append(write)
    for write in writes:
        write.wait()


def correlate(thirds, parts, pick, lags, senders, receivers, partners, limit=60):
    steps, nt = senders[0].shape[0] // 512, len(thirds)
    hbm = pl.BlockSpec(memory_space=pl.ANY)
    sizes = [sum(piece[3] for piece in part) * steps for part in parts]
    ins = [pick, lags, *senders, *receivers, *partners]
    return pl.pallas_call(
        functools.partial(correlate_kernel, thirds, steps, parts),
        out_shape=[jax.ShapeDtypeStruct((n, NLAG, 128), BF16) for n in sizes],
        in_specs=[hbm] * len(ins),
        out_specs=[hbm] * len(sizes),
        scratch_shapes=[pltpu.VMEM((n, NLAG, 128), BF16) for n in sizes]
        + [
            pltpu.VMEM(pick.shape, BF16),
            pltpu.VMEM(lags.shape, BF16),
            pltpu.VMEM((2 + 2 * nt,) + senders[0].shape, BF16),
            pltpu.VMEM((2 * nt, FB, 256, 128), BF16),
            pltpu.VMEM((steps, 1 + nt, 4, 256, 256), BF16),
            pltpu.VMEM((steps, nt, 16, FB, 16, 128), BF16),
            pltpu.SemaphoreType.DMA((4 + 2 * nt + 8 * nt,)),
            pltpu.SemaphoreType.DMA((len(sizes),)),
        ],
        compiler_params=pltpu.CompilerParams(vmem_limit_bytes=limit * MB),
        cost_estimate=pl.CostEstimate(flops=10**6, bytes_accessed=10**6, transcendentals=0),
        name="correlate",
    )(*ins)


def finish_kernel(*refs):
    ins, out = refs[:-1], refs[-1]
    half = pl.program_id(0)

    def total(*xs):
        first = xs[0].astype(F32)
        for x in xs[1:]:
            first = first + x.astype(F32)
        return first.T

    for s in range(STEPS):
        rows = [ref.shape[0] // STEPS for ref in ins]
        g0, k1, k2, y1, xa1, xb1, y2, xa2, xb2 = [
            ref.at[pl.ds(s * n, n)] for ref, n in zip(ins, rows)
        ]

        def put(r, third, value, s=s):
            out[r, s, third * 128 : (third + 1) * 128, :] = value

        @pl.when(half == 0)
        def _():
            for r in range(2):
                put(r, 0, total(g0[r], xa2[r], xb2[r]))
                put(r, 1, total(k1[r], y1[r], xb2[4 + r]))
                put(r, 2, total(k2[r], y1[4 + r], xa2[4 + r]))

        @pl.when(half == 1)
        def _():
            for r in range(2):
                put(r, 0, total(g0[2 + r], xa2[2 + r], xb2[2 + r]))
                put(r, 1, total(k1[2 + r], xb1[r], y2[r]))
                put(r, 2, total(k2[2 + r], xa1[r], y2[2 + r]))


def finish(ins, channels):
    def whole(x):
        return pl.BlockSpec(x.shape, lambda h: (0, 0, 0))

    return pl.pallas_call(
        finish_kernel,
        grid=(2,),
        out_shape=jax.ShapeDtypeStruct((4, STEPS, channels, NLAG), F32),
        in_specs=[whole(x) for x in ins],
        out_specs=pl.BlockSpec((2, STEPS, channels, NLAG), lambda h: (h, 0, 0, 0)),
        compiler_params=pltpu.CompilerParams(vmem_limit_bytes=60 * MB),
        name="finish",
    )(*ins)


def merge_kernel(*refs):
    rows = [ref.shape[0] // STEPS for ref in refs]

    def add(x, y):
        return (x.astype(F32) + y.astype(F32)).astype(BF16)

    for s in range(STEPS):
        g1, g3, k13, k10, k21, k20, y, xa, xb, ua, ub, y2, xa2, xb2 = [
            ref.at[pl.ds(s * n, n)] for ref, n in zip(refs, rows)
        ]
        for r in range(2):
            y2[r] = add(k10[r], xb[2 + r])
            y2[2 + r] = add(k20[r], xa[2 + r])
            xa2[r] = g1[r]
            xa2[2 + r] = add(g1[2 + r], ub[r])
            xa2[4 + r] = add(k21[r], y[6 + r])
            xb2[r] = add(g3[r], ua[r])
            xb2[2 + r] = g3[2 + r]
            xb2[4 + r] = add(k13[r], y[2 + r])


def merge(ins, sizes):
    vmem = pl.BlockSpec(memory_space=pltpu.VMEM)
    return pl.pallas_call(
        merge_kernel,
        out_shape=[jax.ShapeDtypeStruct((n,) + ins[0].shape[1:], BF16) for n in sizes],
        in_specs=[vmem] * len(ins),
        out_specs=[vmem] * len(sizes),
        compiler_params=pltpu.CompilerParams(vmem_limit_bytes=60 * MB),
        name="merge",
    )(*ins)


def on_device(traces, channel_mask, source_blocks):
    windows, segments, channels, length = traces.shape
    traces = traces.reshape(windows * segments, channels, length)
    table = jnp.asarray(dft_rows(length))
    scale = 1.0 / (windows * lax.axis_size("win") * segments)
    lags = jnp.asarray(lag_rows(length, scale))

    def chan_swap(x, bits):
        return lax.ppermute(x, "chan", [(i, i ^ bits) for i in range(16)])

    def win_swap(x, pair):
        bits = pair[0] * 4 + pair[1]
        return lax.ppermute(x, "win", [(i, i ^ bits) for i in range(8)])

    r0, r1, r2, keep0, keep1, send0, send1 = spectra(traces, channel_mask, source_blocks, table)
    p1, p2 = win_swap(r1, PAIRS[1]), win_swap(r2, PAIRS[2])
    part0, part1 = keep0 + chan_swap(send0, 1), keep1 + chan_swap(send1, 1)
    part0, part1 = part0 + chan_swap(part0, 8), part1 + chan_swap(part1, 8)
    pick = pick_rows()
    part0, part1, r0, pick = lax.optimization_barrier((part0, part1, r0, pick))
    p0 = win_swap(r0, PAIRS[0])

    for one, other in ((2, 6), (6, 2)):
        part0, part1 = part0 + chan_swap(part0, one), part1 + chan_swap(part1, other)
    part0, part1, p1, p2 = lax.optimization_barrier((part0, part1, p1, p2))
    part = jnp.concatenate([part0, part1])
    own, *found = [part] + [win_swap(part, pair) for pair in (PAIRS[1], PAIRS[2], PAIRS[0])]
    own = (own, chan_swap(own, 1))
    from_a, from_b = [(half, chan_swap(half, 1)) for half in found[:2]]
    y1, xa1, xb1, k1, k13, k10, k2, k21, k20 = correlate(
        (1, 2), PARTS_12, pick, lags, own + from_a + from_b, (r1, r2), (p1, p2)
    )
    own, from_y, p0, y1, xa1, xb1 = lax.optimization_barrier((own, found[2], p0, y1, xa1, xb1))
    from_y = (from_y, chan_swap(from_y, 1))
    y1, xa1, xb1 = win_swap(y1, (1, 0)), win_swap(xa1, (0, 1)), win_swap(xb1, (0, 3))
    ua, ub, g0, g1, g3 = correlate((0,), PARTS_0, pick, lags, own + from_y, (r0,), (p0,))
    ua, ub = win_swap(ua, (0, 1)), win_swap(ub, (0, 3))
    y2, xa2, xb2 = merge([g1, g3, k13, k10, k21, k20, y1, xa1, xb1, ua, ub], [8, 12, 12])
    y2, xa2, xb2 = win_swap(y2, (1, 0)), win_swap(xa2, (0, 1)), win_swap(xb2, (0, 3))
    return finish([g0, k1, k2, y1, xa1, xb1, y2, xa2, xb2], channels)


def solution(mesh):
    in_specs = (P("win", None, "chan", None), P("chan"), P())
    out_specs = P("win", None, "chan", None)
    return jax.shard_map(
        on_device, mesh=mesh, in_specs=in_specs, out_specs=out_specs, check_vma=False
    )
```

```python
import functools
import math

import jax
import jax.numpy as jnp
import ml_dtypes
import numpy as np
from jax import lax
from jax.experimental import pallas as pl
from jax.experimental.pallas import tpu as pltpu
from jax.sharding import PartitionSpec as P

NF = 128
F_LO = 8
NLAG = 128
VSB = 8
NSRC = 4
STEPS = 2
WATER_LEVEL = 0.05
TINY_ENERGY = 1e-06

FB = 16
BF16 = jnp.bfloat16
F32 = jnp.float32
MB = 2**20

PLACES = ((0, 0), (0, 1), (0, 2), (0, 3), (1, 0), (1, 1), (1, 3))
KEPT = (((0, 0), (0, 1), (0, 2), (0, 3)), ((0, 0), (0, 3), (1, 0), (1, 3)), ((0, 0), (0, 1), (1, 0), (1, 1)))
PAIRS = ((1, 0), (0, 1), (0, 3))
PARTS_12 = (
    ((1, (1, 0), 0, 1), (1, (1, 3), 0, 1), (2, (1, 0), 0, 1), (2, (1, 1), 0, 1)),
    ((2, (0, 1), 1, 3), (2, (1, 1), 1, 3)),
    ((1, (0, 3), 1, 3), (1, (1, 3), 1, 3)),
    ((1, (0, 0), 0, 4),),
    ((1, (0, 3), 0, 1),),
    ((1, (1, 0), 1, 3),),
    ((2, (0, 0), 0, 4),),
    ((2, (0, 1), 0, 1),),
    ((2, (1, 0), 1, 3),),
)
PARTS_0 = (
    ((0, (0, 2), 0, 2),),
    ((0, (0, 2), 2, 2),),
    ((0, (0, 0), 0, 4),),
    ((0, (0, 1), 0, 4),),
    ((0, (0, 3), 0, 4),),
)


def band_rows():
    row = np.arange(2 * NF)
    return F_LO + (row // 16) * 8 + row % 8, (row // 8) % 2


def dft_rows(length):
    bins, part = band_rows()
    t = np.arange(length)
    angle = (t[None, :] * bins[:, None] % length) * (2.0 * math.pi / length)
    taper = 0.5 - 0.5 * np.cos((t + 0.5) * (2.0 * math.pi / length))
    table = np.where(part[:, None] == 0, np.cos(angle), -np.sin(angle)) * taper[None, :]
    return table.astype(np.float32).astype(ml_dtypes.bfloat16)


def lag_rows(length, scale):
    bins, part = band_rows()
    shift = np.arange(NLAG) - NLAG // 2
    angle = (shift[:, None] * bins[None, :] % length) * (2.0 * math.pi / length)
    table = np.where(part[None, :] == 0, np.cos(angle), -np.sin(angle))
    table = table.astype(np.float32).astype(ml_dtypes.bfloat16)
    return (table.astype(np.float32) * scale).astype(ml_dtypes.bfloat16)


def dot(a, b, dims=((1,), (0,))):
    return lax.dot_general(a, b, (dims, ((), ())), preferred_element_type=F32)


def iota(shape, dim):
    return lax.broadcasted_iota(jnp.int32, shape, dim)


def whiten_rows(z, live):
    lanes = z.shape[-1]
    z = z.reshape(FB, 2, 8, lanes)
    re, im = z[:, 0], z[:, 1]
    energy = re * re + im * im
    mean = jnp.sum(jnp.sum(energy, axis=0), axis=0, keepdims=True) * (1.0 / NF)
    factor = lax.rsqrt(energy + WATER_LEVEL * mean[None] + TINY_ENERGY) * live[None]
    out = jnp.concatenate([(re * factor)[:, None], (im * factor)[:, None]], axis=1)
    return out.reshape(FB, 16, lanes).astype(BF16)


def spectra_kernel(blocks_ref, traces_ref, table_ref, mask_ref, *rest):
    thirds, (keep0, keep1, send0, send1) = rest[:3], rest[3:]
    chunk, channels = traces_ref.shape[0], traces_ref.shape[1]
    step = pl.program_id(0)
    live = mask_ref[...].astype(F32)[None]
    for n in range(chunk):
        z = dot(table_ref[...], traces_ref[n], ((1,), (1,)))
        w = whiten_rows(z, live)
        start = pl.multiple_of((step * chunk + n) * 16, 16)
        for third, ref in enumerate(thirds):
            ref[:, pl.ds(start, 16), :] = w[:, :, third * 128 : (third + 1) * 128]

    @pl.when(step == pl.num_programs(0) - 1)
    def _():
        chan = lax.axis_index("chan")
        core = chan & 1
        per_device = channels // VSB
        col = iota((1, 256), 1)
        col_block = (col >> 7) * NSRC + ((col & 31) >> 3)
        want = jnp.full((1, 256), -1, jnp.int32)
        for b in range(STEPS * NSRC):
            block = blocks_ref[b // NSRC, b % NSRC]
            holder = block // per_device
            first = jnp.where(holder == chan, (block - holder * per_device) * VSB, -1000)
            want = jnp.where(col_block == b, first + (col & 7), want)
        row = iota((channels, 256), 0)
        select = [
            (row == jnp.where(((col >> 5) & 3) == hi, want, -1)).astype(F32).astype(BF16)
            for hi in range(4)
        ]
        select = jnp.concatenate(select, axis=0)
        for half, pair in ((core, (keep0, keep1)), (1 - core, (send0, send1))):
            for t in range(2):
                low = half * 2 + t
                left = jnp.concatenate(
                    [ref[hi * 4 + low] for hi in range(4) for ref in thirds], axis=1
                )
                out = dot(left, select).astype(BF16)
                pair[0][t * 256 : (t + 1) * 256, :] = out[:, :128]
                pair[1][t * 256 : (t + 1) * 256, :] = out[:, 128:]


def spectra(traces, mask, blocks, table):
    count, channels, length = traces.shape
    chunk = math.gcd(count, 4)
    smem = pl.BlockSpec(memory_space=pltpu.SMEM)
    third = jax.ShapeDtypeStruct((FB, count * 16, channels // 3), BF16)
    shape = jax.ShapeDtypeStruct((512, 128), BF16)
    return pl.pallas_call(
        spectra_kernel,
        grid=(count // chunk,),
        out_shape=[third] * 3 + [shape] * 4,
        in_specs=[
            smem,
            pl.BlockSpec((chunk, channels, length), lambda n: (n, 0, 0)),
            pl.BlockSpec((2 * NF, length), lambda n: (0, 0)),
            pl.BlockSpec((channels,), lambda n: (0,)),
        ],
        out_specs=[pl.BlockSpec(third.shape, lambda n: (0, 0, 0))] * 3
        + [pl.BlockSpec((512, 128), lambda n: (0, 0))] * 4,
        compiler_params=pltpu.CompilerParams(vmem_limit_bytes=60 * MB),
        cost_estimate=pl.CostEstimate(flops=10**9, bytes_accessed=10**7, transcendentals=0),
        name="spectra",
    )(blocks, traces, table, mask)


def swap_parts(x):
    y = x.astype(F32).reshape(16, 2, 8, x.shape[-1])
    y = jnp.concatenate([-y[:, 1:2], y[:, 0:1]], axis=1)
    return y.reshape(256, x.shape[-1]).astype(BF16)


def pick_kernel(pick):
    win = lax.axis_index("win")
    my_y, my_x = win >> 2, win & 3
    for g, (ey, ex) in enumerate(PLACES):
        row, col = iota((64, 256), 0), iota((64, 256), 1)
        source = ((((my_y ^ ey) * 4) + (my_x ^ ex)) << 2) + (row >> 4)
        key = (((row >> 3) & 1) << 7) + source
        for hi in range(4):
            pick[hi, g * 64 : (g + 1) * 64, :] = (col == key + hi * 32).astype(F32).astype(BF16)


def pick_rows():
    return pl.pallas_call(
        pick_kernel,
        out_shape=jax.ShapeDtypeStruct((4, 64 * len(PLACES), 256), BF16),
        out_specs=pl.BlockSpec(memory_space=pltpu.VMEM),
        cost_estimate=pl.CostEstimate(flops=10**6, bytes_accessed=10**6, transcendentals=0),
        name="pick_rows",
    )()


def spread(rows, right):
    diagonal = ((iota((16, 256), 0) & 7) == (iota((16, 256), 1) & 7)).astype(F32).astype(BF16)
    left = dot(rows, right, ((1,), (1,))).astype(BF16)
    return (left.reshape(-1, 16, 256) * diagonal[None]).reshape(left.shape)


def some(x, third):
    at = [PLACES.index(place) * 64 for place in KEPT[third]]
    return jnp.concatenate([x[i : i + 64] for i in at], axis=0)


def both_parts(both, who, ref, half, steps):
    for s in range(steps):
        for t in range(2):
            at = s * 512 + t * 256
            x = ref[at : at + 256, :]
            both[s, who, half * 2 + t] = jnp.concatenate([x, swap_parts(x)], axis=1)


def quarters(refs, held, sems):
    return [
        [
            pltpu.make_async_copy(
                ref.at[pl.ds(hi * 4, 4)], held.at[i, pl.ds(hi * 4, 4)], sems.at[hi, i]
            )
            for i, ref in enumerate(refs)
        ]
        for hi in range(4)
    ]


def own_kernel(steps, pick_hbm, a_hbm, b_hbm, *rest):
    sources, outs = rest[:3], rest[3:6]
    pick, senders, held, both, stacked, sems, late_sems, out_sems = rest[6:]
    core = lax.axis_index("chan") & 1
    early = [
        pltpu.make_async_copy(src, dst, sems.at[i])
        for i, (src, dst) in enumerate(
            [(a_hbm, senders.at[0]), (b_hbm, senders.at[1]), (pick_hbm, pick)]
        )
    ]
    late = quarters(sources, held, late_sems)
    for copy in early + [copy for group in late for copy in group]:
        copy.start()
    for half in range(2):
        early[half].wait()
        both_parts(both, 0, senders.at[half], half, steps)
    early[2].wait()
    writes = []
    for hi in range(4):
        for copy in late[hi]:
            copy.wait()
        for lo in range(4):
            block = hi * 4 + (((lo >> 1) ^ core) << 1) + (lo & 1)
            own = [spread(pick[hi], both[s, 0, lo]) for s in range(steps)]
            for third in range(3):
                left = jnp.concatenate([some(x, third) for x in own], axis=0)
                out = dot(left, held[third, block]).astype(BF16)
                stacked[third, :, :, block] = out.reshape(steps, 16, 16, 128)
        for third in range(3):
            at = pl.ds(hi * 4, 4)
            write = pltpu.make_async_copy(
                stacked.at[third, :, :, at], outs[third].at[:, :, at], out_sems.at[hi, third]
            )
            write.start()
            writes.append(write)
    for write in writes:
        write.wait()


def correlate_own(pick, senders, receivers):
    steps = senders[0].shape[0] // 512
    hbm = pl.BlockSpec(memory_space=pl.ANY)
    shape = (steps, 16, FB, 16, 128)
    return pl.pallas_call(
        functools.partial(own_kernel, steps),
        out_shape=[jax.ShapeDtypeStruct(shape, BF16)] * 3,
        in_specs=[hbm] * 6,
        out_specs=[hbm] * 3,
        scratch_shapes=[
            pltpu.VMEM(pick.shape, BF16),
            pltpu.VMEM((2,) + senders[0].shape, BF16),
            pltpu.VMEM((3, FB, 256, 128), BF16),
            pltpu.VMEM((steps, 1, 4, 256, 256), BF16),
            pltpu.VMEM((3,) + shape, BF16),
            pltpu.SemaphoreType.DMA((3,)),
            pltpu.SemaphoreType.DMA((4, 3)),
            pltpu.SemaphoreType.DMA((4, 3)),
        ],
        compiler_params=pltpu.CompilerParams(vmem_limit_bytes=24 * MB),
        cost_estimate=pl.CostEstimate(flops=10**6, bytes_accessed=10**6, transcendentals=0),
        name="correlate_own",
    )(pick, *senders, *receivers)


def correlate_kernel(thirds, steps, parts, *rest):
    nt = len(thirds)
    rest = list(rest)
    ins = [rest.pop(0) for _ in range(2 + 2 * nt)]
    partners = [rest.pop(0) for _ in range(nt)]
    sums = [rest.pop(0) for _ in range(nt)]
    outs = [rest.pop(0) for _ in parts]
    results = [rest.pop(0) for _ in parts]
    pick, lag_ref, senders, held, summed, both, stacked, sems, late_sems, out_sems = rest
    core = lax.axis_index("chan") & 1
    targets = [pick, lag_ref] + [senders.at[i] for i in range(2 * nt)]
    targets += [summed.at[i] for i in range(nt)]
    early = [
        pltpu.make_async_copy(src, dst, sems.at[i])
        for i, (src, dst) in enumerate(zip(ins + sums, targets))
    ]
    late = quarters(partners, held, late_sems)
    last = [early[1]] + early[2 + 2 * nt :]
    for copy in early[2 : 2 + 2 * nt] + early[:1] + [c for group in late for c in group] + last:
        copy.start()
    for who in range(nt):
        for half in range(2):
            early[2 + who * 2 + half].wait()
            both_parts(both, who, senders.at[who * 2 + half], half, steps)
    early[0].wait()
    for hi in range(4):
        for copy in late[hi]:
            copy.wait()
        rows = pick[hi]
        for lo in range(4):
            block = hi * 4 + (((lo >> 1) ^ core) << 1) + (lo & 1)
            for i, third in enumerate(thirds):
                left = [spread(some(rows, third), both[s, i, lo]) for s in range(steps)]
                out = dot(jnp.concatenate(left, axis=0), held[i, block]).astype(BF16)
                stacked[i, :, :, block] = out.reshape(steps, 16, 16, 128)
    for copy in last:
        copy.wait()
    lag = jnp.concatenate([lag_ref[...], lag_ref[...]], axis=1)
    writes = []
    for p, (part, result, out) in enumerate(zip(parts, results, outs)):
        wanted = [
            (s, thirds.index(third), KEPT[third].index(where) * 4 + first + r)
            for s in range(steps)
            for third, where, first, amount in part
            for r in range(amount)
        ]
        for k in range(0, len(wanted), 2):
            x = [
                jnp.concatenate([ref[i, s, row].reshape(256, 128) for ref in (summed, stacked)])
                for s, i, row in wanted[k : k + 2]
            ]
            y = dot(lag, jnp.concatenate(x, axis=1)).astype(BF16)
            for j in range(len(x)):
                result[k + j] = y[:, j * 128 : (j + 1) * 128]
        write = pltpu.make_async_copy(result, out, out_sems.at[p])
        write.start()
        writes.append(write)
    for write in writes:
        write.wait()


def correlate(thirds, parts, pick, lags, senders, partners, sums):
    steps, nt = senders[0].shape[0] // 512, len(thirds)
    hbm = pl.BlockSpec(memory_space=pl.ANY)
    sizes = [sum(piece[3] for piece in part) * steps for part in parts]
    ins = [pick, lags, *senders, *partners, *sums]
    return pl.pallas_call(
        functools.partial(correlate_kernel, thirds, steps, parts),
        out_shape=[jax.ShapeDtypeStruct((n, NLAG, 128), BF16) for n in sizes],
        in_specs=[hbm] * len(ins),
        out_specs=[hbm] * len(sizes),
        scratch_shapes=[pltpu.VMEM((n, NLAG, 128), BF16) for n in sizes]
        + [
            pltpu.VMEM(pick.shape, BF16),
            pltpu.VMEM(lags.shape, BF16),
            pltpu.VMEM((2 * nt,) + senders[0].shape, BF16),
            pltpu.VMEM((nt, FB, 256, 128), BF16),
            pltpu.VMEM((nt,) + sums[0].shape, BF16),
            pltpu.VMEM((steps, nt, 4, 256, 256), BF16),
            pltpu.VMEM((nt,) + sums[0].shape, BF16),
            pltpu.SemaphoreType.DMA((2 + 3 * nt,)),
            pltpu.SemaphoreType.DMA((4, nt)),
            pltpu.SemaphoreType.DMA((len(sizes),)),
        ],
        compiler_params=pltpu.CompilerParams(vmem_limit_bytes=24 * MB),
        cost_estimate=pl.CostEstimate(flops=10**6, bytes_accessed=10**6, transcendentals=0),
        name="correlate",
    )(*ins)


def by_step(refs):
    for s in range(STEPS):
        yield [
            ref.at[pl.ds(s * (ref.shape[0] // STEPS), ref.shape[0] // STEPS)] for ref in refs
        ]


def finish_kernel(*refs):
    ins, out = refs[:-1], refs[-1]
    half = pl.program_id(0)

    def total(*xs):
        first = xs[0].astype(F32)
        for x in xs[1:]:
            first = first + x.astype(F32)
        return first.T

    for s, (g0, k1, k2, y1, xa1, xb1, y2, xa2, xb2) in enumerate(by_step(ins)):
        for h in range(2):

            @pl.when(half == h)
            def _():
                for j in range(2):
                    r = 2 * h + j
                    one, two = (y1[0], xb2[4]) if r == 0 else (xb1[r - 1], y2[r - 1])
                    three, four = (y1[2], xa2[4]) if r == 0 else (xa1[r - 1], y2[2 + r])
                    out[j, s, :128, :] = total(g0[r], xa2[r], xb2[r])
                    out[j, s, 128:256, :] = total(k1[r], one, two)
                    out[j, s, 256:, :] = total(k2[r], three, four)


def finish(ins, channels):
    def whole(x):
        return pl.BlockSpec(x.shape, lambda h: (0, 0, 0))

    return pl.pallas_call(
        finish_kernel,
        grid=(2,),
        out_shape=jax.ShapeDtypeStruct((4, STEPS, channels, NLAG), F32),
        in_specs=[whole(x) for x in ins],
        out_specs=pl.BlockSpec((2, STEPS, channels, NLAG), lambda h: (h, 0, 0, 0)),
        compiler_params=pltpu.CompilerParams(vmem_limit_bytes=FIN * MB),
        name="finish",
    )(*ins)


FIN = 16


def add(x, y):
    return (x.astype(F32) + y.astype(F32)).astype(BF16)


def merge_thirds_kernel(*refs):
    for k13, k10, k21, k20, y, xa, xb, y2, m21, m13 in by_step(refs):
        for r in range(3):
            y2[r] = add(k10[r], xb[3 + r])
            y2[3 + r] = add(k20[r], xa[3 + r])
        m21[0] = add(k21[0], y[3])
        m13[0] = add(k13[0], y[1])


def merge_ring_kernel(*refs):
    for g1, g3, ua, ub, m21, m13, xa2, xb2 in by_step(refs):
        for r in range(2):
            xa2[r] = g1[r]
            xa2[2 + r] = add(g1[2 + r], ub[r])
            xb2[r] = add(g3[r], ua[r])
            xb2[2 + r] = g3[2 + r]
        xa2[4] = m21[0]
        xb2[4] = m13[0]


def merge(kernel, ins, sizes):
    vmem = pl.BlockSpec(memory_space=pltpu.VMEM)
    return pl.pallas_call(
        kernel,
        out_shape=[jax.ShapeDtypeStruct((n * STEPS,) + ins[0].shape[1:], BF16) for n in sizes],
        in_specs=[vmem] * len(ins),
        out_specs=[vmem] * len(sizes),
        compiler_params=pltpu.CompilerParams(vmem_limit_bytes=FIN * MB),
        name="merge",
    )(*ins)


def on_device(traces, channel_mask, source_blocks):
    windows, segments, channels, length = traces.shape
    traces = traces.reshape(windows * segments, channels, length)
    table = jnp.asarray(dft_rows(length))
    scale = 1.0 / (windows * lax.axis_size("win") * segments)
    lags = jnp.asarray(lag_rows(length, scale))

    def chan_swap(x, bits):
        return lax.ppermute(x, "chan", [(i, i ^ bits) for i in range(16)])

    def win_swap(x, pair):
        bits = pair[0] * 4 + pair[1]
        return lax.ppermute(x, "win", [(i, i ^ bits) for i in range(8)])

    r0, r1, r2, keep0, keep1, send0, send1 = spectra(traces, channel_mask, source_blocks, table)
    p1, p2 = win_swap(r1, PAIRS[1]), win_swap(r2, PAIRS[2])
    part0, part1 = keep0 + chan_swap(send0, 1), keep1 + chan_swap(send1, 1)
    pick = pick_rows()
    for one, other in ((8, 2), (2, 8), (6, 6)):
        part0, part1 = part0 + chan_swap(part0, one), part1 + chan_swap(part1, other)
        if one == 8:
            part1, pick = lax.optimization_barrier((part1, pick))
        if other == 8:
            part0, part1, r0 = lax.optimization_barrier((part0, part1, r0))
            p0 = win_swap(r0, PAIRS[0])
    part0, part1, p1, p2 = lax.optimization_barrier((part0, part1, p1, p2))
    part = jnp.concatenate([part0, part1])
    from_a, from_b, from_y = [win_swap(part, pair) for pair in (PAIRS[1], PAIRS[2], PAIRS[0])]
    s0, s1, s2 = correlate_own(pick, (part, chan_swap(part, 1)), (r0, r1, r2))
    from_a, from_b, s0, s1, s2 = lax.optimization_barrier((from_a, from_b, s0, s1, s2))
    senders = [x for half in (from_a, from_b) for x in (half, chan_swap(half, 1))]
    y1, xa1, xb1, k1, k13, k10, k2, k21, k20 = correlate(
        (1, 2), PARTS_12, pick, lags, senders, (p1, p2), (s1, s2)
    )
    from_y, p0, y1, xa1, xb1 = lax.optimization_barrier((from_y, p0, y1, xa1, xb1))
    y1, xa1, xb1 = win_swap(y1, (1, 0)), win_swap(xa1, (0, 1)), win_swap(xb1, (0, 3))
    senders = [from_y, chan_swap(from_y, 1)]
    ua, ub, g0, g1, g3 = correlate((0,), PARTS_0, pick, lags, senders, (p0,), (s0,))
    ua, ub = win_swap(ua, (0, 1)), win_swap(ub, (0, 3))
    y2, m21, m13 = merge(merge_thirds_kernel, [k13, k10, k21, k20, y1, xa1, xb1], [6, 1, 1])
    y2 = win_swap(y2, (1, 0))
    xa2, xb2 = merge(merge_ring_kernel, [g1, g3, ua, ub, m21, m13], [5, 5])
    xa2, xb2 = win_swap(xa2, (0, 1)), win_swap(xb2, (0, 3))
    return finish([g0, k1, k2, y1, xa1, xb1, y2, xa2, xb2], channels)


def solution(mesh):
    in_specs = (P("win", None, "chan", None), P("chan"), P())
    out_specs = P("win", None, "chan", None)
    return jax.shard_map(
        on_device, mesh=mesh, in_specs=in_specs, out_specs=out_specs, check_vma=False
    )
```

```python
import functools
import math

import jax
import jax.numpy as jnp
import ml_dtypes
import numpy as np
from jax import lax
from jax.experimental import pallas as pl
from jax.experimental.pallas import tpu as pltpu
from jax.sharding import PartitionSpec as P

NF = 128
F_LO = 8
NLAG = 128
VSB = 8
NSRC = 4
STEPS = 2
WATER_LEVEL = 0.05
TINY_ENERGY = 1e-06

FB = 16
BF16 = jnp.bfloat16
F32 = jnp.float32
MB = 2**20

PLACES = ((0, 0), (0, 1), (0, 2), (0, 3), (1, 0), (1, 1), (1, 3))
KEPT = (((0, 0), (0, 1), (0, 2), (0, 3)), ((0, 0), (0, 3), (1, 0), (1, 3)), ((0, 0), (0, 1), (1, 0), (1, 1)))
PAIRS = ((1, 0), (0, 1), (0, 3))
PARTS_12 = (
    ((1, (1, 0), 0, 1), (1, (1, 3), 0, 1), (2, (1, 0), 0, 1), (2, (1, 1), 0, 1)),
    ((2, (0, 1), 1, 3), (2, (1, 1), 1, 3)),
    ((1, (0, 3), 1, 3), (1, (1, 3), 1, 3)),
    ((1, (0, 0), 0, 4),),
    ((1, (0, 3), 0, 1),),
    ((1, (1, 0), 1, 3),),
    ((2, (0, 0), 0, 4),),
    ((2, (0, 1), 0, 1),),
    ((2, (1, 0), 1, 3),),
)
PARTS_0 = (
    ((0, (0, 2), 0, 2),),
    ((0, (0, 2), 2, 2),),
    ((0, (0, 0), 0, 4),),
    ((0, (0, 1), 0, 4),),
    ((0, (0, 3), 0, 4),),
)


def band_rows():
    row = np.arange(2 * NF)
    return F_LO + (row // 16) * 8 + row % 8, (row // 8) % 2


def dft_rows(length):
    bins, part = band_rows()
    t = np.arange(length)
    angle = (t[None, :] * bins[:, None] % length) * (2.0 * math.pi / length)
    taper = 0.5 - 0.5 * np.cos((t + 0.5) * (2.0 * math.pi / length))
    table = np.where(part[:, None] == 0, np.cos(angle), -np.sin(angle)) * taper[None, :]
    return table.astype(np.float32).astype(ml_dtypes.bfloat16)


def lag_rows(length, scale):
    bins, part = band_rows()
    shift = np.arange(NLAG) - NLAG // 2
    angle = (shift[:, None] * bins[None, :] % length) * (2.0 * math.pi / length)
    table = np.where(part[None, :] == 0, np.cos(angle), -np.sin(angle))
    table = table.astype(np.float32).astype(ml_dtypes.bfloat16)
    return (table.astype(np.float32) * scale).astype(ml_dtypes.bfloat16)


def dot(a, b, dims=((1,), (0,))):
    return lax.dot_general(a, b, (dims, ((), ())), preferred_element_type=F32)


def iota(shape, dim):
    return lax.broadcasted_iota(jnp.int32, shape, dim)


def whiten_rows(z, live):
    lanes = z.shape[-1]
    z = z.reshape(FB, 2, 8, lanes)
    re, im = z[:, 0], z[:, 1]
    energy = re * re + im * im
    mean = jnp.sum(jnp.sum(energy, axis=0), axis=0, keepdims=True) * (1.0 / NF)
    factor = lax.rsqrt(energy + WATER_LEVEL * mean[None] + TINY_ENERGY) * live[None]
    out = jnp.concatenate([(re * factor)[:, None], (im * factor)[:, None]], axis=1)
    return out.reshape(FB, 16, lanes).astype(BF16)


def spectra_kernel(blocks_ref, traces_ref, table_ref, mask_ref, *rest):
    thirds, parts, (xbuf, held, select, sems, out_sems) = rest[:3], rest[3:7], rest[7:]
    keep0, keep1, send0, send1 = parts
    count, channels = xbuf.shape[0], xbuf.shape[1]
    turns = sems.shape[0]
    chunk = count // turns
    copies = [
        pltpu.make_async_copy(
            traces_ref.at[pl.ds(i * chunk, chunk)], xbuf.at[pl.ds(i * chunk, chunk)], sems.at[i]
        )
        for i in range(turns)
    ]
    for copy in copies:
        copy.start()
    chan = lax.axis_index("chan")
    core = chan & 1
    per_device = channels // VSB
    col = iota((1, 256), 1)
    col_block = (col >> 7) * NSRC + ((col & 31) >> 3)
    want = jnp.full((1, 256), -1, jnp.int32)
    for b in range(STEPS * NSRC):
        block = blocks_ref[b // NSRC, b % NSRC]
        holder = block // per_device
        first = jnp.where(holder == chan, (block - holder * per_device) * VSB, -1000)
        want = jnp.where(col_block == b, first + (col & 7), want)
    row = iota((channels, 256), 0)
    for hi in range(4):
        wanted = jnp.where(((col >> 5) & 3) == hi, want, -1)
        select[hi * channels : (hi + 1) * channels, :] = (row == wanted).astype(F32).astype(BF16)
    live = mask_ref[...].astype(F32)[None]
    writes = []
    for i in range(turns):
        copies[i].wait()
        for n in range(i * chunk, (i + 1) * chunk):
            w = whiten_rows(dot(table_ref[...], xbuf[n], ((1,), (1,))), live)
            for third in range(3):
                held[third, :, n * 16 : (n + 1) * 16, :] = w[:, :, third * 128 : (third + 1) * 128]
        if i % 2 == 1:
            at = pl.ds((i - 1) * chunk * 16, 2 * chunk * 16)
            for third in range(3):
                write = pltpu.make_async_copy(
                    held.at[third, :, at], thirds[third].at[:, at], out_sems.at[i // 2, third]
                )
                write.start()
                writes.append(write)
    for half, pair in ((core, (keep0, keep1)), (1 - core, (send0, send1))):
        for t in range(2):
            low = half * 2 + t
            left = [held[third, hi * 4 + low] for hi in range(4) for third in range(3)]
            out = dot(jnp.concatenate(left, axis=1), select[...]).astype(BF16)
            pair[0][t * 256 : (t + 1) * 256, :] = out[:, :128]
            pair[1][t * 256 : (t + 1) * 256, :] = out[:, 128:]
    for write in writes:
        write.wait()


def spectra(traces, mask, blocks, table):
    count, channels, length = traces.shape
    vmem, hbm = pl.BlockSpec(memory_space=pltpu.VMEM), pl.BlockSpec(memory_space=pl.ANY)
    third = jax.ShapeDtypeStruct((FB, count * 16, channels // 3), BF16)
    shape = jax.ShapeDtypeStruct((512, 128), BF16)
    return pl.pallas_call(
        spectra_kernel,
        out_shape=[third] * 3 + [shape] * 4,
        in_specs=[pl.BlockSpec(memory_space=pltpu.SMEM), hbm, vmem, vmem],
        out_specs=[hbm] * 3 + [vmem] * 4,
        scratch_shapes=[
            pltpu.VMEM(traces.shape, BF16),
            pltpu.VMEM((3,) + third.shape, BF16),
            pltpu.VMEM((4 * channels, 256), BF16),
            pltpu.SemaphoreType.DMA((8,)),
            pltpu.SemaphoreType.DMA((4, 3)),
        ],
        compiler_params=pltpu.CompilerParams(vmem_limit_bytes=60 * MB),
        cost_estimate=pl.CostEstimate(flops=10**9, bytes_accessed=10**7, transcendentals=0),
        name="spectra",
    )(blocks, traces, table, mask)


def swap_parts(x):
    y = x.astype(F32).reshape(16, 2, 8, x.shape[-1])
    y = jnp.concatenate([-y[:, 1:2], y[:, 0:1]], axis=1)
    return y.reshape(256, x.shape[-1]).astype(BF16)


def pick_kernel(pick, pick_sent):
    win = lax.axis_index("win")
    my_y, my_x = win >> 2, win & 3
    for g, (ey, ex) in enumerate(PLACES):
        row, col = iota((64, 256), 0), iota((64, 256), 1)
        source = ((((my_y ^ ey) * 4) + (my_x ^ ex)) << 2) + (row >> 4)
        key = (((row >> 3) & 1) << 7) + source
        for hi in range(4):
            pick[hi, g * 64 : (g + 1) * 64, :] = (col == key + hi * 32).astype(F32).astype(BF16)
    row, col = iota((256, 256), 0), iota((256, 256), 1)
    key = (((row >> 3) & 1) << 7) + (row >> 4)
    for t in range(2):
        for hi in range(4):
            at = t * 4 + hi
            pick_sent[at] = (col == key + at * 16).astype(F32).astype(BF16)


def pick_rows():
    vmem = pl.BlockSpec(memory_space=pltpu.VMEM)
    shapes = (4, 64 * len(PLACES), 256), (8, 256, 256)
    return pl.pallas_call(
        pick_kernel,
        out_shape=[jax.ShapeDtypeStruct(shape, BF16) for shape in shapes],
        out_specs=[vmem] * 2,
        cost_estimate=pl.CostEstimate(flops=10**6, bytes_accessed=10**6, transcendentals=0),
        name="pick_rows",
    )()


def narrow_kernel(*refs):
    ins, outs = refs[:STEPS], refs[STEPS:]
    win = lax.axis_index("win")
    my_y, my_x = win >> 2, win & 3
    row, col = iota((256, 128), 0), iota((1, 128), 1)
    for third, out in enumerate(outs):
        want = jnp.zeros((1, 128), jnp.int32)
        for p, (ey, ex) in enumerate(KEPT[third]):
            at_y, at_x = my_y ^ PAIRS[third][0] ^ ey, my_x ^ PAIRS[third][1] ^ ex
            want = jnp.where(((col >> 2) & 3) == p, (at_y * 4 + at_x) * 4, want)
        select = (row == want + (col & 3) + (col >> 4) * 32).astype(F32).astype(BF16)
        for s, x in enumerate(ins):
            x = jnp.concatenate([x[:256, :], x[256:, :]], axis=1)
            out[s * 256 : (s + 1) * 256, :] = dot(x, select).astype(BF16)


def narrow(parts):
    vmem = pl.BlockSpec(memory_space=pltpu.VMEM)
    return pl.pallas_call(
        narrow_kernel,
        out_shape=[jax.ShapeDtypeStruct((256 * STEPS, 128), BF16)] * 3,
        in_specs=[vmem] * STEPS,
        out_specs=[vmem] * 3,
        compiler_params=pltpu.CompilerParams(vmem_limit_bytes=16 * MB),
        cost_estimate=pl.CostEstimate(flops=10**6, bytes_accessed=10**6, transcendentals=0),
        name="narrow",
    )(*parts)


def spread(rows, right):
    diagonal = ((iota((16, 256), 0) & 7) == (iota((16, 256), 1) & 7)).astype(F32).astype(BF16)
    left = dot(rows, right, ((1,), (1,))).astype(BF16)
    return (left.reshape(-1, 16, 256) * diagonal[None]).reshape(left.shape)


def some(x, third):
    at = [PLACES.index(place) * 64 for place in KEPT[third]]
    return jnp.concatenate([x[i : i + 64] for i in at], axis=0)


def both_parts(both, who, ref, half, steps):
    for place, s in enumerate(steps):
        for t in range(2):
            at = s * 512 + t * 256
            x = ref[at : at + 256, :]
            both[place, who, half * 2 + t] = jnp.concatenate([x, swap_parts(x)], axis=1)


def own_kernel(steps, pick, a, b, *rest):
    sources, outs, both = rest[:3], rest[3:6], rest[6]
    core = lax.axis_index("chan") & 1
    for half, ref in enumerate((a, b)):
        both_parts(both, 0, ref, half, range(steps))
    for hi in range(4):
        for lo in range(4):
            block = hi * 4 + (((lo >> 1) ^ core) << 1) + (lo & 1)
            own = [spread(pick[hi], both[s, 0, lo]) for s in range(steps)]
            for third in range(3):
                left = jnp.concatenate([some(x, third) for x in own], axis=0)
                out = dot(left, sources[third][block]).astype(BF16)
                outs[third][:, :, block] = out.reshape(steps, 16, 16, 128)


def correlate_own(pick, senders, receivers):
    steps = senders[0].shape[0] // 512
    vmem = pl.BlockSpec(memory_space=pltpu.VMEM)
    shape = (steps, 16, FB, 16, 128)
    return pl.pallas_call(
        functools.partial(own_kernel, steps),
        out_shape=[jax.ShapeDtypeStruct(shape, BF16)] * 3,
        in_specs=[vmem] * 6,
        out_specs=[vmem] * 3,
        scratch_shapes=[pltpu.VMEM((steps, 1, 4, 256, 256), BF16)],
        compiler_params=pltpu.CompilerParams(vmem_limit_bytes=24 * MB),
        cost_estimate=pl.CostEstimate(flops=10**6, bytes_accessed=10**6, transcendentals=0),
        name="correlate_own",
    )(pick, *senders, *receivers)


def correlate_kernel(thirds, steps, parts, pick, lag_ref, *rest):
    nt = len(thirds)
    senders, partners, sums = rest[: 2 * nt], rest[2 * nt : 3 * nt], rest[3 * nt : 4 * nt]
    outs, (both, stacked) = rest[4 * nt : 4 * nt + len(parts)], rest[4 * nt + len(parts) :]
    core = lax.axis_index("chan") & 1
    for who in range(nt):
        for half in range(2):
            for place, s in enumerate(steps):
                x = senders[who * 2 + half][s * 256 : (s + 1) * 256, :]
                both[place, who, half] = jnp.concatenate([x, swap_parts(x)], axis=1)
    for hi in range(4):
        for lo in range(4):
            rows = pick[(lo & 1) * 4 + hi]
            block = hi * 4 + (((lo >> 1) ^ core) << 1) + (lo & 1)
            for i, third in enumerate(thirds):
                left = [spread(rows, both[s, i, lo >> 1]) for s in range(len(steps))]
                out = dot(jnp.concatenate(left, axis=0), partners[i][block]).astype(BF16)
                stacked[i, :, :, block] = out.reshape(len(steps), 16, 16, 128)
    lag = jnp.concatenate([lag_ref[...], lag_ref[...]], axis=1)
    for part, out in zip(parts, outs):
        wanted = [
            (s, thirds.index(third), KEPT[third].index(where) * 4 + first + r)
            for s in range(len(steps))
            for third, where, first, amount in part
            for r in range(amount)
        ]
        for k in range(0, len(wanted), 2):
            x = [
                jnp.concatenate(
                    [sums[i][steps[s], row].reshape(256, 128), stacked[i, s, row].reshape(256, 128)]
                )
                for s, i, row in wanted[k : k + 2]
            ]
            y = dot(lag, jnp.concatenate(x, axis=1)).astype(BF16)
            for j in range(len(x)):
                out[k + j] = y[:, j * 128 : (j + 1) * 128]


def correlate(thirds, parts, steps, pick, lags, senders, partners, sums):
    nt, count = len(thirds), len(steps)
    vmem = pl.BlockSpec(memory_space=pltpu.VMEM)
    sizes = [sum(piece[3] for piece in part) * count for part in parts]
    ins = [pick, lags, *senders, *partners, *sums]
    return pl.pallas_call(
        functools.partial(correlate_kernel, thirds, steps, parts),
        out_shape=[jax.ShapeDtypeStruct((n, NLAG, 128), BF16) for n in sizes],
        in_specs=[vmem] * len(ins),
        out_specs=[vmem] * len(sizes),
        scratch_shapes=[
            pltpu.VMEM((count, nt, 2, 256, 256), BF16),
            pltpu.VMEM((nt, count) + sums[0].shape[1:], BF16),
        ],
        compiler_params=pltpu.CompilerParams(vmem_limit_bytes=24 * MB),
        cost_estimate=pl.CostEstimate(flops=10**6, bytes_accessed=10**6, transcendentals=0),
        name="correlate",
    )(*ins)


def by_step(refs):
    for s in range(STEPS):
        rows = [ref.shape[0] // STEPS for ref in refs]
        yield [ref.at[pl.ds(s * n, n)] for ref, n in zip(refs, rows)]


def finish_kernel(*refs):
    ins, out = refs[:-1], refs[-1]
    half = pl.program_id(0)

    def total(*xs):
        first = xs[0].astype(F32)
        for x in xs[1:]:
            first = first + x.astype(F32)
        return first.T

    for s, (k1, k2, y1, xa1, xb1, g0, y2, xa2, xb2, ma, mb) in enumerate(by_step(ins)):
        for h in range(2):

            @pl.when(half == h)
            def _():
                for j in range(2):
                    r = 2 * h + j
                    one, two = (y1[0], mb[0]) if r == 0 else (xb1[r - 1], y2[r - 1])
                    three, four = (y1[2], ma[0]) if r == 0 else (xa1[r - 1], y2[2 + r])
                    out[j, s, :128, :] = total(g0[r], xa2[r], xb2[r])
                    out[j, s, 128:256, :] = total(k1[r], one, two)
                    out[j, s, 256:, :] = total(k2[r], three, four)


def finish(ins, channels):
    def whole(x):
        return pl.BlockSpec(x.shape, lambda h: (0, 0, 0))

    return pl.pallas_call(
        finish_kernel,
        grid=(2,),
        out_shape=jax.ShapeDtypeStruct((4, STEPS, channels, NLAG), F32),
        in_specs=[whole(x) for x in ins],
        out_specs=pl.BlockSpec((2, STEPS, channels, NLAG), lambda h: (h, 0, 0, 0)),
        compiler_params=pltpu.CompilerParams(vmem_limit_bytes=16 * MB),
        name="finish",
    )(*ins)


def add(x, y):
    return (x.astype(F32) + y.astype(F32)).astype(BF16)


def merge_once_kernel(*refs):
    for k13, k21, y, ma, mb in by_step(refs):
        ma[0] = add(k21[0], y[3])
        mb[0] = add(k13[0], y[1])


def merge_thirds_kernel(*refs):
    for k10, k20, xa, xb, y2 in by_step(refs):
        for r in range(3):
            y2[r] = add(k10[r], xb[3 + r])
            y2[3 + r] = add(k20[r], xa[3 + r])


def merge_ring_kernel(*refs):
    for g1, g3, ua, ub, xa2, xb2 in by_step(refs):
        for r in range(2):
            xa2[r] = g1[r]
            xa2[2 + r] = add(g1[2 + r], ub[r])
            xb2[r] = add(g3[r], ua[r])
            xb2[2 + r] = g3[2 + r]


def merge(kernel, ins, sizes):
    vmem = pl.BlockSpec(memory_space=pltpu.VMEM)
    return pl.pallas_call(
        kernel,
        out_shape=[jax.ShapeDtypeStruct((n * STEPS,) + ins[0].shape[1:], BF16) for n in sizes],
        in_specs=[vmem] * len(ins),
        out_specs=[vmem] * len(sizes),
        compiler_params=pltpu.CompilerParams(vmem_limit_bytes=16 * MB),
        name="merge",
    )(*ins)


def on_device(traces, channel_mask, source_blocks):
    windows, segments, channels, length = traces.shape
    traces = traces.reshape(windows * segments, channels, length)
    table = jnp.asarray(dft_rows(length))
    scale = 1.0 / (windows * lax.axis_size("win") * segments)
    lags = jnp.asarray(lag_rows(length, scale))

    def chan_swap(x, bits):
        return lax.ppermute(x, "chan", [(i, i ^ bits) for i in range(16)])

    def win_swap(x, pair):
        bits = pair[0] * 4 + pair[1]
        return lax.ppermute(x, "win", [(i, i ^ bits) for i in range(8)])

    r0, r1, r2, keep0, keep1, send0, send1 = spectra(traces, channel_mask, source_blocks, table)
    p1, p2 = win_swap(r1, PAIRS[1]), win_swap(r2, PAIRS[2])
    part0, part1 = keep0 + chan_swap(send0, 1), keep1 + chan_swap(send1, 1)
    pick, pick_sent = pick_rows()
    for one, other in ((8, 2), (2, 8), (6, 6)):
        part0, part1 = part0 + chan_swap(part0, one), part1 + chan_swap(part1, other)
        if other == 8:
            part0, part1, r0, pick, pick_sent = lax.optimization_barrier(
                (part0, part1, r0, pick, pick_sent)
            )
            p0 = win_swap(r0, PAIRS[0])
    part0, part1, p1, p2 = lax.optimization_barrier((part0, part1, p1, p2))
    part = jnp.concatenate([part0, part1])
    to_y, to_a, to_b = narrow([part0, part1])
    from_a, from_b = win_swap(to_a, PAIRS[1]), win_swap(to_b, PAIRS[2])
    from_y = win_swap(to_y, PAIRS[0])
    s0, s1, s2 = correlate_own(pick, (part, chan_swap(part, 1)), (r0, r1, r2))
    from_a, from_b, s0, s1, s2 = lax.optimization_barrier((from_a, from_b, s0, s1, s2))
    senders = [x for half in (from_a, from_b) for x in (half, chan_swap(half, 1))]
    y, xa, xb, k1, k13, k10, k2, k21, k20 = correlate(
        (1, 2), PARTS_12, (0, 1), pick_sent, lags, senders, (p1, p2), (s1, s2)
    )
    from_y, p0, y, xa, xb = lax.optimization_barrier((from_y, p0, y, xa, xb))
    y1, xa1, xb1 = win_swap(y, (1, 0)), win_swap(xa, (0, 1)), win_swap(xb, (0, 3))
    senders = [from_y, chan_swap(from_y, 1)]
    ua, ub, g0, g1, g3 = correlate((0,), PARTS_0, (0, 1), pick_sent, lags, senders, (p0,), (s0,))
    ua, ub = win_swap(ua, (0, 1)), win_swap(ub, (0, 3))
    ma, mb = merge(merge_once_kernel, [k13, k21, y1], [1, 1])
    xa1, xb1, ma, mb = lax.optimization_barrier((xa1, xb1, ma, mb))
    (y2,) = merge(merge_thirds_kernel, [k10, k20, xa1, xb1], [6])
    y2 = win_swap(y2, (1, 0))
    ma, mb = win_swap(ma, (0, 1)), win_swap(mb, (0, 3))
    xa2, xb2 = merge(merge_ring_kernel, [g1, g3, ua, ub], [4, 4])
    xa2, xb2 = win_swap(xa2, (0, 1)), win_swap(xb2, (0, 3))
    return finish([k1, k2, y1, xa1, xb1, g0, y2, xa2, xb2, ma, mb], channels)


def solution(mesh):
    in_specs = (P("win", None, "chan", None), P("chan"), P())
    out_specs = P("win", None, "chan", None)
    return jax.shard_map(
        on_device, mesh=mesh, in_specs=in_specs, out_specs=out_specs, check_vma=False
    )
```

```python
import functools
import math

import jax
import jax.numpy as jnp
import ml_dtypes
import numpy as np
from jax import lax
from jax.experimental import pallas as pl
from jax.experimental.pallas import tpu as pltpu
from jax.sharding import PartitionSpec as P

NF = 128
F_LO = 8
NLAG = 128
VSB = 8
NSRC = 4
STEPS = 2
WATER_LEVEL = 0.05
TINY_ENERGY = 1e-06

FB = 16
BF16 = jnp.bfloat16
TURNS = 4
F32 = jnp.float32
MB = 2**20

PLACES = ((0, 0), (0, 1), (0, 2), (0, 3), (1, 0), (1, 1), (1, 3))
KEPT = (((0, 0), (0, 1), (0, 2), (0, 3)), ((0, 0), (0, 3), (1, 0), (1, 3)), ((0, 0), (0, 1), (1, 0), (1, 1)))
PAIRS = ((1, 0), (0, 1), (0, 3))
PARTS_12 = (
    ((1, (1, 0), 0, 1), (1, (1, 3), 0, 1), (2, (1, 0), 0, 1), (2, (1, 1), 0, 1)),
    ((2, (0, 1), 1, 3), (2, (1, 1), 1, 3)),
    ((1, (0, 3), 1, 3), (1, (1, 3), 1, 3)),
    ((1, (0, 0), 0, 4),),
    ((1, (0, 3), 0, 1),),
    ((1, (1, 0), 1, 3),),
    ((2, (0, 0), 0, 4),),
    ((2, (0, 1), 0, 1),),
    ((2, (1, 0), 1, 3),),
)
PARTS_0 = (
    ((0, (0, 2), 0, 2),),
    ((0, (0, 2), 2, 2),),
    ((0, (0, 0), 0, 4),),
    ((0, (0, 1), 0, 4),),
    ((0, (0, 3), 0, 4),),
)


def band_rows():
    row = np.arange(2 * NF)
    return F_LO + (row // 16) * 8 + row % 8, (row // 8) % 2


def dft_rows(length):
    bins, part = band_rows()
    t = np.arange(length)
    angle = (t[None, :] * bins[:, None] % length) * (2.0 * math.pi / length)
    taper = 0.5 - 0.5 * np.cos((t + 0.5) * (2.0 * math.pi / length))
    table = np.where(part[:, None] == 0, np.cos(angle), -np.sin(angle)) * taper[None, :]
    return table.astype(np.float32).astype(ml_dtypes.bfloat16)


def lag_rows(length, scale):
    bins, part = band_rows()
    shift = np.arange(NLAG) - NLAG // 2
    angle = (shift[:, None] * bins[None, :] % length) * (2.0 * math.pi / length)
    table = np.where(part[None, :] == 0, np.cos(angle), -np.sin(angle))
    table = table.astype(np.float32).astype(ml_dtypes.bfloat16)
    return (table.astype(np.float32) * scale).astype(ml_dtypes.bfloat16)


def dot(a, b, dims=((1,), (0,))):
    return lax.dot_general(a, b, (dims, ((), ())), preferred_element_type=F32)


def iota(shape, dim):
    return lax.broadcasted_iota(jnp.int32, shape, dim)


def whiten_rows(z, live):
    lanes = z.shape[-1]
    z = z.reshape(FB, 2, 8, lanes)
    re, im = z[:, 0], z[:, 1]
    energy = re * re + im * im
    mean = jnp.sum(jnp.sum(energy, axis=0), axis=0, keepdims=True) * (1.0 / NF)
    factor = lax.rsqrt(energy + WATER_LEVEL * mean[None] + TINY_ENERGY) * live[None]
    out = jnp.concatenate([(re * factor)[:, None], (im * factor)[:, None]], axis=1)
    return out.reshape(FB, 16, lanes).astype(BF16)


def spectra_kernel(blocks_ref, traces_ref, table_ref, mask_ref, *rest):
    thirds, parts, (xbuf, held, select, sems, out_sems) = rest[:3], rest[3:7], rest[7:]
    keep0, keep1, send0, send1 = parts
    count, channels = xbuf.shape[0], xbuf.shape[1]
    turns = sems.shape[0]
    chunk = count // turns

    def read(i):
        at = pl.ds(i * chunk, chunk)
        return pltpu.make_async_copy(traces_ref.at[at], xbuf.at[at], sems.at[i])

    def write(i, third):
        at = pl.ds(pl.multiple_of(i * chunk * 16, 16), chunk * 16)
        return pltpu.make_async_copy(
            held.at[third, :, at], thirds[third].at[:, at], out_sems.at[i, third]
        )

    for i in range(turns):
        read(i).start()
    chan = lax.axis_index("chan")
    core = chan & 1
    per_device = channels // VSB
    col = iota((1, 256), 1)
    col_block = (col >> 7) * NSRC + ((col & 31) >> 3)
    want = jnp.full((1, 256), -1, jnp.int32)
    for b in range(STEPS * NSRC):
        block = blocks_ref[b // NSRC, b % NSRC]
        holder = block // per_device
        first = jnp.where(holder == chan, (block - holder * per_device) * VSB, -1000)
        want = jnp.where(col_block == b, first + (col & 7), want)
    row = iota((channels, 256), 0)
    for hi in range(4):
        wanted = jnp.where(((col >> 5) & 3) == hi, want, -1)
        select[hi * channels : (hi + 1) * channels, :] = (row == wanted).astype(F32).astype(BF16)
    live = mask_ref[...].astype(F32)[None]

    def turn(i, carry):
        read(i).wait()
        for k in range(chunk):
            n = i * chunk + k
            w = whiten_rows(dot(table_ref[...], xbuf[n], ((1,), (1,))), live)
            at = pl.ds(pl.multiple_of(n * 16, 16), 16)
            for third in range(3):
                held[third, :, at, :] = w[:, :, third * 128 : (third + 1) * 128]
        for third in range(3):
            write(i, third).start()
        return carry

    lax.fori_loop(0, turns, turn, 0)
    for half, pair in ((core, (keep0, keep1)), (1 - core, (send0, send1))):
        for t in range(2):
            low = half * 2 + t
            left = [held[third, hi * 4 + low] for hi in range(4) for third in range(3)]
            out = dot(jnp.concatenate(left, axis=1), select[...]).astype(BF16)
            pair[0][t * 256 : (t + 1) * 256, :] = out[:, :128]
            pair[1][t * 256 : (t + 1) * 256, :] = out[:, 128:]
    for i in range(turns):
        for third in range(3):
            write(i, third).wait()


def spectra(traces, mask, blocks, table):
    count, channels, length = traces.shape
    vmem, hbm = pl.BlockSpec(memory_space=pltpu.VMEM), pl.BlockSpec(memory_space=pl.ANY)
    third = jax.ShapeDtypeStruct((FB, count * 16, channels // 3), BF16)
    shape = jax.ShapeDtypeStruct((512, 128), BF16)
    return pl.pallas_call(
        spectra_kernel,
        out_shape=[third] * 3 + [shape] * 4,
        in_specs=[pl.BlockSpec(memory_space=pltpu.SMEM), hbm, vmem, vmem],
        out_specs=[hbm] * 3 + [vmem] * 4,
        scratch_shapes=[
            pltpu.VMEM(traces.shape, BF16),
            pltpu.VMEM((3,) + third.shape, BF16),
            pltpu.VMEM((4 * channels, 256), BF16),
            pltpu.SemaphoreType.DMA((TURNS,)),
            pltpu.SemaphoreType.DMA((TURNS, 3)),
        ],
        compiler_params=pltpu.CompilerParams(vmem_limit_bytes=60 * MB),
        cost_estimate=pl.CostEstimate(flops=10**9, bytes_accessed=10**7, transcendentals=0),
        name="spectra",
    )(blocks, traces, table, mask)


def swap_parts(x):
    y = x.astype(F32).reshape(16, 2, 8, x.shape[-1])
    y = jnp.concatenate([-y[:, 1:2], y[:, 0:1]], axis=1)
    return y.reshape(256, x.shape[-1]).astype(BF16)


def pick_kernel(pick, pick_sent):
    win = lax.axis_index("win")
    my_y, my_x = win >> 2, win & 3
    for g, (ey, ex) in enumerate(PLACES):
        row, col = iota((64, 256), 0), iota((64, 256), 1)
        source = ((((my_y ^ ey) * 4) + (my_x ^ ex)) << 2) + (row >> 4)
        key = (((row >> 3) & 1) << 7) + source
        for hi in range(4):
            pick[hi, g * 64 : (g + 1) * 64, :] = (col == key + hi * 32).astype(F32).astype(BF16)
    row, col = iota((256, 256), 0), iota((256, 256), 1)
    key = (((row >> 3) & 1) << 7) + (row >> 4)
    for t in range(2):
        for hi in range(4):
            at = t * 4 + hi
            pick_sent[at] = (col == key + at * 16).astype(F32).astype(BF16)


def pick_rows():
    vmem = pl.BlockSpec(memory_space=pltpu.VMEM)
    shapes = (4, 64 * len(PLACES), 256), (8, 256, 256)
    return pl.pallas_call(
        pick_kernel,
        out_shape=[jax.ShapeDtypeStruct(shape, BF16) for shape in shapes],
        out_specs=[vmem] * 2,
        compiler_params=pltpu.CompilerParams(vmem_limit_bytes=16 * MB),
        cost_estimate=pl.CostEstimate(flops=10**6, bytes_accessed=10**6, transcendentals=0),
        name="pick_rows",
    )()


def narrow_kernel(*refs):
    ins, outs = refs[:STEPS], refs[STEPS:]
    win = lax.axis_index("win")
    my_y, my_x = win >> 2, win & 3
    row, col = iota((256, 128), 0), iota((1, 128), 1)
    for third, out in enumerate(outs):
        want = jnp.zeros((1, 128), jnp.int32)
        for p, (ey, ex) in enumerate(KEPT[third]):
            at_y, at_x = my_y ^ PAIRS[third][0] ^ ey, my_x ^ PAIRS[third][1] ^ ex
            want = jnp.where(((col >> 2) & 3) == p, (at_y * 4 + at_x) * 4, want)
        select = (row == want + (col & 3) + (col >> 4) * 32).astype(F32).astype(BF16)
        for s, x in enumerate(ins):
            x = jnp.concatenate([x[:256, :], x[256:, :]], axis=1)
            out[s * 256 : (s + 1) * 256, :] = dot(x, select).astype(BF16)


def narrow(parts):
    vmem = pl.BlockSpec(memory_space=pltpu.VMEM)
    return pl.pallas_call(
        narrow_kernel,
        out_shape=[jax.ShapeDtypeStruct((256 * STEPS, 128), BF16)] * 3,
        in_specs=[vmem] * STEPS,
        out_specs=[vmem] * 3,
        compiler_params=pltpu.CompilerParams(vmem_limit_bytes=16 * MB),
        cost_estimate=pl.CostEstimate(flops=10**6, bytes_accessed=10**6, transcendentals=0),
        name="narrow",
    )(*parts)


def spread(rows, right):
    diagonal = ((iota((16, 256), 0) & 7) == (iota((16, 256), 1) & 7)).astype(F32).astype(BF16)
    left = dot(rows, right, ((1,), (1,))).astype(BF16)
    return (left.reshape(-1, 16, 256) * diagonal[None]).reshape(left.shape)


def some(x, third):
    at = [PLACES.index(place) * 64 for place in KEPT[third]]
    return jnp.concatenate([x[i : i + 64] for i in at], axis=0)


def both_parts(both, who, ref, half, steps):
    for place, s in enumerate(steps):
        for t in range(2):
            at = s * 512 + t * 256
            x = ref[at : at + 256, :]
            both[place, who, half * 2 + t] = jnp.concatenate([x, swap_parts(x)], axis=1)


def own_kernel(steps, pick, a, b, *rest):
    sources, outs, both = rest[:3], rest[3:6], rest[6]
    core = lax.axis_index("chan") & 1
    for half, ref in enumerate((a, b)):
        both_parts(both, 0, ref, half, range(steps))
    for hi in range(4):
        for lo in range(4):
            block = hi * 4 + (((lo >> 1) ^ core) << 1) + (lo & 1)
            own = [spread(pick[hi], both[s, 0, lo]) for s in range(steps)]
            for third in range(3):
                left = jnp.concatenate([some(x, third) for x in own], axis=0)
                out = dot(left, sources[third][block]).astype(BF16)
                outs[third][:, :, block] = out.reshape(steps, 16, 16, 128)


def correlate_own(pick, senders, receivers):
    steps = senders[0].shape[0] // 512
    vmem = pl.BlockSpec(memory_space=pltpu.VMEM)
    shape = (steps, 16, FB, 16, 128)
    return pl.pallas_call(
        functools.partial(own_kernel, steps),
        out_shape=[jax.ShapeDtypeStruct(shape, BF16)] * 3,
        in_specs=[vmem] * 6,
        out_specs=[vmem] * 3,
        scratch_shapes=[pltpu.VMEM((steps, 1, 4, 256, 256), BF16)],
        compiler_params=pltpu.CompilerParams(vmem_limit_bytes=24 * MB),
        cost_estimate=pl.CostEstimate(flops=10**6, bytes_accessed=10**6, transcendentals=0),
        name="correlate_own",
    )(pick, *senders, *receivers)


def correlate_kernel(thirds, steps, parts, pick, lag_ref, *rest):
    nt = len(thirds)
    senders, partners, sums = rest[: 2 * nt], rest[2 * nt : 3 * nt], rest[3 * nt : 4 * nt]
    outs, (both, stacked) = rest[4 * nt : 4 * nt + len(parts)], rest[4 * nt + len(parts) :]
    core = lax.axis_index("chan") & 1
    for who in range(nt):
        for half in range(2):
            for place, s in enumerate(steps):
                x = senders[who * 2 + half][s * 256 : (s + 1) * 256, :]
                both[place, who, half] = jnp.concatenate([x, swap_parts(x)], axis=1)
    for hi in range(4):
        for lo in range(4):
            rows = pick[(lo & 1) * 4 + hi]
            block = hi * 4 + (((lo >> 1) ^ core) << 1) + (lo & 1)
            for i, third in enumerate(thirds):
                left = [spread(rows, both[s, i, lo >> 1]) for s in range(len(steps))]
                out = dot(jnp.concatenate(left, axis=0), partners[i][block])
                out = out.reshape(len(steps), 16, 16, 128)
                for place, s in enumerate(steps):
                    both_groups = out[place] + sums[i][s, :, block].astype(F32)
                    stacked[i, place, :, block] = both_groups.astype(BF16)
    lag = lag_ref[...]
    for part, out in zip(parts, outs):
        wanted = [
            (s, thirds.index(third), KEPT[third].index(where) * 4 + first + r)
            for s in range(len(steps))
            for third, where, first, amount in part
            for r in range(amount)
        ]
        for k in range(0, len(wanted), 2):
            x = [stacked[i, s, row].reshape(256, 128) for s, i, row in wanted[k : k + 2]]
            y = dot(lag, jnp.concatenate(x, axis=1)).astype(BF16)
            for j in range(len(x)):
                out[k + j] = y[:, j * 128 : (j + 1) * 128]


def correlate(thirds, parts, steps, pick, lags, senders, partners, sums):
    nt, count = len(thirds), len(steps)
    vmem = pl.BlockSpec(memory_space=pltpu.VMEM)
    sizes = [sum(piece[3] for piece in part) * count for part in parts]
    ins = [pick, lags, *senders, *partners, *sums]
    return pl.pallas_call(
        functools.partial(correlate_kernel, thirds, steps, parts),
        out_shape=[jax.ShapeDtypeStruct((n, NLAG, 128), BF16) for n in sizes],
        in_specs=[vmem] * len(ins),
        out_specs=[vmem] * len(sizes),
        scratch_shapes=[
            pltpu.VMEM((count, nt, 2, 256, 256), BF16),
            pltpu.VMEM((nt, count) + sums[0].shape[1:], BF16),
        ],
        compiler_params=pltpu.CompilerParams(vmem_limit_bytes=24 * MB),
        cost_estimate=pl.CostEstimate(flops=10**6, bytes_accessed=10**6, transcendentals=0),
        name="correlate",
    )(*ins)


def by_step(refs):
    for s in range(STEPS):
        rows = [ref.shape[0] // STEPS for ref in refs]
        yield [ref.at[pl.ds(s * n, n)] for ref, n in zip(refs, rows)]


def finish_kernel(*refs):
    ins, out = refs[:-1], refs[-1]
    half = pl.program_id(0)

    def total(*xs):
        first = xs[0].astype(F32)
        for x in xs[1:]:
            first = first + x.astype(F32)
        return first.T

    for s, (k1, k2, y1, xa1, xb1, g0, y2, xa2, xb2, ma, mb) in enumerate(by_step(ins)):
        for h in range(2):

            @pl.when(half == h)
            def _():
                for j in range(2):
                    r = 2 * h + j
                    one, two = (y1[0], mb[0]) if r == 0 else (xb1[r - 1], y2[r - 1])
                    three, four = (y1[2], ma[0]) if r == 0 else (xa1[r - 1], y2[2 + r])
                    out[j, s, :128, :] = total(g0[r], xa2[r], xb2[r])
                    out[j, s, 128:256, :] = total(k1[r], one, two)
                    out[j, s, 256:, :] = total(k2[r], three, four)


def finish(ins, channels):
    def whole(x):
        return pl.BlockSpec(x.shape, lambda h: (0, 0, 0))

    return pl.pallas_call(
        finish_kernel,
        grid=(2,),
        out_shape=jax.ShapeDtypeStruct((4, STEPS, channels, NLAG), F32),
        in_specs=[whole(x) for x in ins],
        out_specs=pl.BlockSpec((2, STEPS, channels, NLAG), lambda h: (h, 0, 0, 0)),
        compiler_params=pltpu.CompilerParams(vmem_limit_bytes=16 * MB),
        name="finish",
    )(*ins)


def add(x, y):
    return (x.astype(F32) + y.astype(F32)).astype(BF16)


def merge_once_kernel(*refs):
    for k13, k21, y, ma, mb in by_step(refs):
        ma[0] = add(k21[0], y[3])
        mb[0] = add(k13[0], y[1])


def merge_thirds_kernel(*refs):
    for k10, k20, xa, xb, y2 in by_step(refs):
        for r in range(3):
            y2[r] = add(k10[r], xb[3 + r])
            y2[3 + r] = add(k20[r], xa[3 + r])


def merge_ring_kernel(*refs):
    for g1, g3, ua, ub, xa2, xb2 in by_step(refs):
        for r in range(2):
            xa2[r] = g1[r]
            xa2[2 + r] = add(g1[2 + r], ub[r])
            xb2[r] = add(g3[r], ua[r])
            xb2[2 + r] = g3[2 + r]


def merge(kernel, ins, sizes):
    vmem = pl.BlockSpec(memory_space=pltpu.VMEM)
    return pl.pallas_call(
        kernel,
        out_shape=[jax.ShapeDtypeStruct((n * STEPS,) + ins[0].shape[1:], BF16) for n in sizes],
        in_specs=[vmem] * len(ins),
        out_specs=[vmem] * len(sizes),
        compiler_params=pltpu.CompilerParams(vmem_limit_bytes=16 * MB),
        name="merge",
    )(*ins)


def on_device(traces, channel_mask, source_blocks):
    windows, segments, channels, length = traces.shape
    traces = traces.reshape(windows * segments, channels, length)
    table = jnp.asarray(dft_rows(length))
    scale = 1.0 / (windows * lax.axis_size("win") * segments)
    lags = jnp.asarray(lag_rows(length, scale))

    def chan_swap(x, bits):
        return lax.ppermute(x, "chan", [(i, i ^ bits) for i in range(16)])

    def win_swap(x, pair):
        bits = pair[0] * 4 + pair[1]
        return lax.ppermute(x, "win", [(i, i ^ bits) for i in range(8)])

    r0, r1, r2, keep0, keep1, send0, send1 = spectra(traces, channel_mask, source_blocks, table)
    p1, p2 = win_swap(r1, PAIRS[1]), win_swap(r2, PAIRS[2])
    part0, part1 = keep0 + chan_swap(send0, 1), keep1 + chan_swap(send1, 1)
    pick, pick_sent = pick_rows()
    for one, other in ((8, 2), (2, 8), (6, 6)):
        part0, part1 = part0 + chan_swap(part0, one), part1 + chan_swap(part1, other)
        if other == 8:
            part0, part1, r0, pick, pick_sent = lax.optimization_barrier(
                (part0, part1, r0, pick, pick_sent)
            )
            p0 = win_swap(r0, PAIRS[0])
    part0, part1, p1, p2 = lax.optimization_barrier((part0, part1, p1, p2))
    part = jnp.concatenate([part0, part1])
    to_y, to_a, to_b = narrow([part0, part1])
    from_a, from_b = win_swap(to_a, PAIRS[1]), win_swap(to_b, PAIRS[2])
    from_y = win_swap(to_y, PAIRS[0])
    s0, s1, s2 = correlate_own(pick, (part, chan_swap(part, 1)), (r0, r1, r2))
    from_a, from_b, s0, s1, s2 = lax.optimization_barrier((from_a, from_b, s0, s1, s2))
    senders = [x for half in (from_a, from_b) for x in (half, chan_swap(half, 1))]
    y, xa, xb, k1, k13, k10, k2, k21, k20 = correlate(
        (1, 2), PARTS_12, (0, 1), pick_sent, lags, senders, (p1, p2), (s1, s2)
    )
    from_y, p0, y, xa, xb = lax.optimization_barrier((from_y, p0, y, xa, xb))
    y1, xa1, xb1 = win_swap(y, (1, 0)), win_swap(xa, (0, 1)), win_swap(xb, (0, 3))
    senders = [from_y, chan_swap(from_y, 1)]
    ua, ub, g0, g1, g3 = correlate((0,), PARTS_0, (0, 1), pick_sent, lags, senders, (p0,), (s0,))
    ua, ub = win_swap(ua, (0, 1)), win_swap(ub, (0, 3))
    ma, mb = merge(merge_once_kernel, [k13, k21, y1], [1, 1])
    xa1, xb1, ma, mb = lax.optimization_barrier((xa1, xb1, ma, mb))
    (y2,) = merge(merge_thirds_kernel, [k10, k20, xa1, xb1], [6])
    y2 = win_swap(y2, (1, 0))
    ma, mb = win_swap(ma, (0, 1)), win_swap(mb, (0, 3))
    xa2, xb2 = merge(merge_ring_kernel, [g1, g3, ua, ub], [4, 4])
    xa2, xb2 = win_swap(xa2, (0, 1)), win_swap(xb2, (0, 3))
    return finish([k1, k2, y1, xa1, xb1, g0, y2, xa2, xb2, ma, mb], channels)


def solution(mesh):
    in_specs = (P("win", None, "chan", None), P("chan"), P())
    out_specs = P("win", None, "chan", None)
    return jax.shard_map(
        on_device, mesh=mesh, in_specs=in_specs, out_specs=out_specs, check_vma=False
    )
```

```python
import functools
import math

import jax
import jax.numpy as jnp
import ml_dtypes
import numpy as np
from jax import lax
from jax.experimental import pallas as pl
from jax.experimental.pallas import tpu as pltpu
from jax.sharding import PartitionSpec as P

NF = 128
F_LO = 8
NLAG = 128
VSB = 8
NSRC = 4
STEPS = 2
WATER_LEVEL = 0.05
TINY_ENERGY = 1e-06

FB = 16
BF16 = jnp.bfloat16
TURNS = 4
F32 = jnp.float32
MB = 2**20

PLACES = ((0, 0), (0, 1), (0, 2), (0, 3), (1, 0), (1, 1), (1, 3))
KEPT = (((0, 0), (0, 1), (0, 2), (0, 3)), ((0, 0), (0, 3), (1, 0), (1, 3)), ((0, 0), (0, 1), (1, 0), (1, 1)))
PAIRS = ((1, 0), (0, 1), (0, 3))
PARTS_12 = (
    ((1, (1, 0), 0, 1), (1, (1, 3), 0, 1), (2, (1, 0), 0, 1), (2, (1, 1), 0, 1)),
    ((2, (0, 1), 1, 3), (2, (1, 1), 1, 3)),
    ((1, (0, 3), 1, 3), (1, (1, 3), 1, 3)),
    ((1, (0, 0), 0, 4),),
    ((1, (0, 3), 0, 1),),
    ((1, (1, 0), 1, 3),),
    ((2, (0, 0), 0, 4),),
    ((2, (0, 1), 0, 1),),
    ((2, (1, 0), 1, 3),),
)
PARTS_0 = (
    ((0, (0, 2), 0, 2),),
    ((0, (0, 2), 2, 2),),
    ((0, (0, 0), 0, 4),),
    ((0, (0, 1), 0, 4),),
    ((0, (0, 3), 0, 4),),
)


def band_rows():
    row = np.arange(2 * NF)
    return F_LO + (row // 16) * 8 + row % 8, (row // 8) % 2


def dft_rows(length):
    bins, part = band_rows()
    t = np.arange(length)
    angle = (t[None, :] * bins[:, None] % length) * (2.0 * math.pi / length)
    taper = 0.5 - 0.5 * np.cos((t + 0.5) * (2.0 * math.pi / length))
    table = np.where(part[:, None] == 0, np.cos(angle), -np.sin(angle)) * taper[None, :]
    return table.astype(np.float32).astype(ml_dtypes.bfloat16)


def lag_rows(length, scale):
    bins, part = band_rows()
    shift = np.arange(NLAG) - NLAG // 2
    angle = (shift[:, None] * bins[None, :] % length) * (2.0 * math.pi / length)
    table = np.where(part[None, :] == 0, np.cos(angle), -np.sin(angle))
    table = table.astype(np.float32).astype(ml_dtypes.bfloat16)
    return (table.astype(np.float32) * scale).astype(ml_dtypes.bfloat16)


def dot(a, b, dims=((1,), (0,))):
    return lax.dot_general(a, b, (dims, ((), ())), preferred_element_type=F32)


def iota(shape, dim):
    return lax.broadcasted_iota(jnp.int32, shape, dim)


def whiten_rows(z, live):
    lanes = z.shape[-1]
    z = z.reshape(FB, 2, 8, lanes)
    re, im = z[:, 0], z[:, 1]
    energy = re * re + im * im
    mean = jnp.sum(jnp.sum(energy, axis=0), axis=0, keepdims=True) * (1.0 / NF)
    factor = lax.rsqrt(energy + WATER_LEVEL * mean[None] + TINY_ENERGY) * live[None]
    out = jnp.concatenate([(re * factor)[:, None], (im * factor)[:, None]], axis=1)
    return out.reshape(FB, 16, lanes).astype(BF16)


def spectra_kernel(blocks_ref, traces_ref, table_ref, mask_ref, *rest):
    thirds, parts, (xbuf, held, select, sems, out_sems) = rest[:3], rest[3:7], rest[7:]
    keep0, keep1, send0, send1 = parts
    count, channels = xbuf.shape[0], xbuf.shape[1]
    turns = sems.shape[0]
    chunk = count // turns

    def read(i):
        at = pl.ds(i * chunk, chunk)
        return pltpu.make_async_copy(traces_ref.at[at], xbuf.at[at], sems.at[i])

    def write(i, third):
        at = pl.ds(pl.multiple_of(i * chunk * 16, 16), chunk * 16)
        return pltpu.make_async_copy(
            held.at[third, :, at], thirds[third].at[:, at], out_sems.at[i, third]
        )

    for i in range(turns):
        read(i).start()
    chan = lax.axis_index("chan")
    core = chan & 1
    per_device = channels // VSB
    col = iota((1, 256), 1)
    col_block = (col >> 7) * NSRC + ((col & 31) >> 3)
    want = jnp.full((1, 256), -1, jnp.int32)
    for b in range(STEPS * NSRC):
        block = blocks_ref[b // NSRC, b % NSRC]
        holder = block // per_device
        first = jnp.where(holder == chan, (block - holder * per_device) * VSB, -1000)
        want = jnp.where(col_block == b, first + (col & 7), want)
    row = iota((channels, 256), 0)
    for hi in range(4):
        wanted = jnp.where(((col >> 5) & 3) == hi, want, -1)
        select[hi * channels : (hi + 1) * channels, :] = (row == wanted).astype(F32).astype(BF16)
    live = mask_ref[...].astype(F32)[None]

    def turn(i, carry):
        read(i).wait()
        for k in range(chunk):
            n = i * chunk + k
            w = whiten_rows(dot(table_ref[...], xbuf[n], ((1,), (1,))), live)
            at = pl.ds(pl.multiple_of(n * 16, 16), 16)
            for third in range(3):
                held[third, :, at, :] = w[:, :, third * 128 : (third + 1) * 128]
        for third in range(3):
            write(i, third).start()
        return carry

    lax.fori_loop(0, turns, turn, 0)
    left = []
    for half in (core, 1 - core):
        for t in range(2):
            low = half * 2 + t
            some_rows = [held[third, hi * 4 + low] for hi in range(4) for third in range(3)]
            left.append(jnp.concatenate(some_rows, axis=1))
    out = dot(jnp.concatenate(left, axis=0), select[...]).astype(BF16)
    for k, (first, second) in enumerate(((keep0, keep1), (send0, send1))):
        first[...] = out[k * 512 : (k + 1) * 512, :128]
        second[...] = out[k * 512 : (k + 1) * 512, 128:]
    for i in range(turns):
        for third in range(3):
            write(i, third).wait()


def spectra(traces, mask, blocks, table):
    count, channels, length = traces.shape
    vmem, hbm = pl.BlockSpec(memory_space=pltpu.VMEM), pl.BlockSpec(memory_space=pl.ANY)
    third = jax.ShapeDtypeStruct((FB, count * 16, channels // 3), BF16)
    shape = jax.ShapeDtypeStruct((512, 128), BF16)
    return pl.pallas_call(
        spectra_kernel,
        out_shape=[third] * 3 + [shape] * 4,
        in_specs=[pl.BlockSpec(memory_space=pltpu.SMEM), hbm, vmem, vmem],
        out_specs=[hbm] * 3 + [vmem] * 4,
        scratch_shapes=[
            pltpu.VMEM(traces.shape, BF16),
            pltpu.VMEM((3,) + third.shape, BF16),
            pltpu.VMEM((4 * channels, 256), BF16),
            pltpu.SemaphoreType.DMA((TURNS,)),
            pltpu.SemaphoreType.DMA((TURNS, 3)),
        ],
        compiler_params=pltpu.CompilerParams(vmem_limit_bytes=60 * MB),
        cost_estimate=pl.CostEstimate(flops=10**9, bytes_accessed=10**7, transcendentals=0),
        name="spectra",
    )(blocks, traces, table, mask)


def swap_parts(x):
    y = x.astype(F32).reshape(16, 2, 8, x.shape[-1])
    y = jnp.concatenate([-y[:, 1:2], y[:, 0:1]], axis=1)
    return y.reshape(256, x.shape[-1]).astype(BF16)


def pick_kernel(pick, pick_sent):
    win = lax.axis_index("win")
    my_y, my_x = win >> 2, win & 3
    for g, (ey, ex) in enumerate(PLACES):
        row, col = iota((64, 256), 0), iota((64, 256), 1)
        source = ((((my_y ^ ey) * 4) + (my_x ^ ex)) << 2) + (row >> 4)
        key = (((row >> 3) & 1) << 7) + source
        for hi in range(4):
            pick[hi, g * 64 : (g + 1) * 64, :] = (col == key + hi * 32).astype(F32).astype(BF16)
    row, col = iota((256, 256), 0), iota((256, 256), 1)
    key = (((row >> 3) & 1) << 7) + (row >> 4)
    for t in range(2):
        for hi in range(4):
            at = t * 4 + hi
            pick_sent[at] = (col == key + at * 16).astype(F32).astype(BF16)


def pick_rows():
    vmem = pl.BlockSpec(memory_space=pltpu.VMEM)
    shapes = (4, 64 * len(PLACES), 256), (8, 256, 256)
    return pl.pallas_call(
        pick_kernel,
        out_shape=[jax.ShapeDtypeStruct(shape, BF16) for shape in shapes],
        out_specs=[vmem] * 2,
        compiler_params=pltpu.CompilerParams(vmem_limit_bytes=16 * MB),
        cost_estimate=pl.CostEstimate(flops=10**6, bytes_accessed=10**6, transcendentals=0),
        name="pick_rows",
    )()


def narrow_kernel(*refs):
    ins, outs = refs[:STEPS], refs[STEPS:]
    win = lax.axis_index("win")
    my_y, my_x = win >> 2, win & 3
    row, col = iota((256, 128), 0), iota((1, 128), 1)
    for third, out in enumerate(outs):
        want = jnp.zeros((1, 128), jnp.int32)
        for p, (ey, ex) in enumerate(KEPT[third]):
            at_y, at_x = my_y ^ PAIRS[third][0] ^ ey, my_x ^ PAIRS[third][1] ^ ex
            want = jnp.where(((col >> 2) & 3) == p, (at_y * 4 + at_x) * 4, want)
        select = (row == want + (col & 3) + (col >> 4) * 32).astype(F32).astype(BF16)
        for s, x in enumerate(ins):
            x = jnp.concatenate([x[:256, :], x[256:, :]], axis=1)
            out[s * 256 : (s + 1) * 256, :] = dot(x, select).astype(BF16)


def narrow(parts):
    vmem = pl.BlockSpec(memory_space=pltpu.VMEM)
    return pl.pallas_call(
        narrow_kernel,
        out_shape=[jax.ShapeDtypeStruct((256 * STEPS, 128), BF16)] * 3,
        in_specs=[vmem] * STEPS,
        out_specs=[vmem] * 3,
        compiler_params=pltpu.CompilerParams(vmem_limit_bytes=16 * MB),
        cost_estimate=pl.CostEstimate(flops=10**6, bytes_accessed=10**6, transcendentals=0),
        name="narrow",
    )(*parts)


def spread(rows, right):
    diagonal = ((iota((16, 256), 0) & 7) == (iota((16, 256), 1) & 7)).astype(F32).astype(BF16)
    left = dot(rows, right, ((1,), (1,))).astype(BF16)
    return (left.reshape(-1, 16, 256) * diagonal[None]).reshape(left.shape)


def some(x, third):
    at = [PLACES.index(place) * 64 for place in KEPT[third]]
    return jnp.concatenate([x[i : i + 64] for i in at], axis=0)


def both_parts(both, who, ref, half, steps):
    for place, s in enumerate(steps):
        for t in range(2):
            at = s * 512 + t * 256
            x = ref[at : at + 256, :]
            both[place, who, half * 2 + t] = jnp.concatenate([x, swap_parts(x)], axis=1)


def own_kernel(steps, pick, a, b, *rest):
    sources, outs, both = rest[:3], rest[3:6], rest[6]
    core = lax.axis_index("chan") & 1
    for half, ref in enumerate((a, b)):
        both_parts(both, 0, ref, half, range(steps))
    for hi in range(4):
        for lo in range(4):
            block = hi * 4 + (((lo >> 1) ^ core) << 1) + (lo & 1)
            own = [spread(pick[hi], both[s, 0, lo]) for s in range(steps)]
            for third in range(3):
                left = jnp.concatenate([some(x, third) for x in own], axis=0)
                out = dot(left, sources[third][block]).astype(BF16)
                outs[third][:, :, block] = out.reshape(steps, 16, 16, 128)


def correlate_own(pick, senders, receivers):
    steps = senders[0].shape[0] // 512
    vmem = pl.BlockSpec(memory_space=pltpu.VMEM)
    shape = (steps, 16, FB, 16, 128)
    return pl.pallas_call(
        functools.partial(own_kernel, steps),
        out_shape=[jax.ShapeDtypeStruct(shape, BF16)] * 3,
        in_specs=[vmem] * 6,
        out_specs=[vmem] * 3,
        scratch_shapes=[pltpu.VMEM((steps, 1, 4, 256, 256), BF16)],
        compiler_params=pltpu.CompilerParams(vmem_limit_bytes=24 * MB),
        cost_estimate=pl.CostEstimate(flops=10**6, bytes_accessed=10**6, transcendentals=0),
        name="correlate_own",
    )(pick, *senders, *receivers)


def correlate_kernel(thirds, steps, parts, pick, lag_ref, *rest):
    nt = len(thirds)
    senders, partners, sums = rest[: 2 * nt], rest[2 * nt : 3 * nt], rest[3 * nt : 4 * nt]
    outs, (both, stacked) = rest[4 * nt : 4 * nt + len(parts)], rest[4 * nt + len(parts) :]
    core = lax.axis_index("chan") & 1
    for who in range(nt):
        for half in range(2):
            for place, s in enumerate(steps):
                x = senders[who * 2 + half][s * 256 : (s + 1) * 256, :]
                both[place, who, half] = jnp.concatenate([x, swap_parts(x)], axis=1)
    for hi in range(4):
        for lo in range(4):
            rows = pick[(lo & 1) * 4 + hi]
            block = hi * 4 + (((lo >> 1) ^ core) << 1) + (lo & 1)
            for i, third in enumerate(thirds):
                left = [spread(rows, both[s, i, lo >> 1]) for s in range(len(steps))]
                out = dot(jnp.concatenate(left, axis=0), partners[i][block])
                out = out.reshape(len(steps), 16, 16, 128)
                for place, s in enumerate(steps):
                    both_groups = out[place] + sums[i][s, :, block].astype(F32)
                    stacked[i, place, :, block] = both_groups.astype(BF16)
    lag = lag_ref[...]
    for part, out in zip(parts, outs):
        wanted = [
            (s, thirds.index(third), KEPT[third].index(where) * 4 + first + r)
            for s in range(len(steps))
            for third, where, first, amount in part
            for r in range(amount)
        ]
        for k in range(0, len(wanted), 2):
            x = [stacked[i, s, row].reshape(256, 128) for s, i, row in wanted[k : k + 2]]
            y = dot(lag, jnp.concatenate(x, axis=1)).astype(BF16)
            for j in range(len(x)):
                out[k + j] = y[:, j * 128 : (j + 1) * 128]


def correlate(thirds, parts, steps, pick, lags, senders, partners, sums):
    nt, count = len(thirds), len(steps)
    vmem = pl.BlockSpec(memory_space=pltpu.VMEM)
    sizes = [sum(piece[3] for piece in part) * count for part in parts]
    ins = [pick, lags, *senders, *partners, *sums]
    return pl.pallas_call(
        functools.partial(correlate_kernel, thirds, steps, parts),
        out_shape=[jax.ShapeDtypeStruct((n, NLAG, 128), BF16) for n in sizes],
        in_specs=[vmem] * len(ins),
        out_specs=[vmem] * len(sizes),
        scratch_shapes=[
            pltpu.VMEM((count, nt, 2, 256, 256), BF16),
            pltpu.VMEM((nt, count) + sums[0].shape[1:], BF16),
        ],
        compiler_params=pltpu.CompilerParams(vmem_limit_bytes=24 * MB),
        cost_estimate=pl.CostEstimate(flops=10**6, bytes_accessed=10**6, transcendentals=0),
        name="correlate",
    )(*ins)


def by_step(refs):
    for s in range(STEPS):
        rows = [ref.shape[0] // STEPS for ref in refs]
        yield [ref.at[pl.ds(s * n, n)] for ref, n in zip(refs, rows)]


def finish_kernel(*refs):
    ins, out = refs[:-1], refs[-1]
    half = pl.program_id(0)

    def total(*xs):
        first = xs[0].astype(F32)
        for x in xs[1:]:
            first = first + x.astype(F32)
        return first.T

    for s, (k1, k2, y1, xa1, xb1, g0, y2, xa2, xb2, ma, mb) in enumerate(by_step(ins)):
        for h in range(2):

            @pl.when(half == h)
            def _():
                for j in range(2):
                    r = 2 * h + j
                    one, two = (y1[0], mb[0]) if r == 0 else (xb1[r - 1], y2[r - 1])
                    three, four = (y1[2], ma[0]) if r == 0 else (xa1[r - 1], y2[2 + r])
                    out[j, s, :128, :] = total(g0[r], xa2[r], xb2[r])
                    out[j, s, 128:256, :] = total(k1[r], one, two)
                    out[j, s, 256:, :] = total(k2[r], three, four)


def finish(ins, channels):
    def whole(x):
        return pl.BlockSpec(x.shape, lambda h: (0, 0, 0))

    return pl.pallas_call(
        finish_kernel,
        grid=(2,),
        out_shape=jax.ShapeDtypeStruct((4, STEPS, channels, NLAG), F32),
        in_specs=[whole(x) for x in ins],
        out_specs=pl.BlockSpec((2, STEPS, channels, NLAG), lambda h: (h, 0, 0, 0)),
        compiler_params=pltpu.CompilerParams(vmem_limit_bytes=16 * MB),
        name="finish",
    )(*ins)


def add(x, y):
    return (x.astype(F32) + y.astype(F32)).astype(BF16)


def merge_once_kernel(*refs):
    for k13, k21, y, ma, mb in by_step(refs):
        ma[0] = add(k21[0], y[3])
        mb[0] = add(k13[0], y[1])


def merge_thirds_kernel(*refs):
    for k10, k20, xa, xb, y2 in by_step(refs):
        for r in range(3):
            y2[r] = add(k10[r], xb[3 + r])
            y2[3 + r] = add(k20[r], xa[3 + r])


def merge_ring_kernel(*refs):
    for g1, g3, ua, ub, xa2, xb2 in by_step(refs):
        for r in range(2):
            xa2[r] = g1[r]
            xa2[2 + r] = add(g1[2 + r], ub[r])
            xb2[r] = add(g3[r], ua[r])
            xb2[2 + r] = g3[2 + r]


def merge(kernel, ins, sizes):
    vmem = pl.BlockSpec(memory_space=pltpu.VMEM)
    return pl.pallas_call(
        kernel,
        out_shape=[jax.ShapeDtypeStruct((n * STEPS,) + ins[0].shape[1:], BF16) for n in sizes],
        in_specs=[vmem] * len(ins),
        out_specs=[vmem] * len(sizes),
        compiler_params=pltpu.CompilerParams(vmem_limit_bytes=16 * MB),
        name="merge",
    )(*ins)


def on_device(traces, channel_mask, source_blocks):
    windows, segments, channels, length = traces.shape
    traces = traces.reshape(windows * segments, channels, length)
    table = jnp.asarray(dft_rows(length))
    scale = 1.0 / (windows * lax.axis_size("win") * segments)
    lags = jnp.asarray(lag_rows(length, scale))

    def chan_swap(x, bits):
        return lax.ppermute(x, "chan", [(i, i ^ bits) for i in range(16)])

    def win_swap(x, pair):
        bits = pair[0] * 4 + pair[1]
        return lax.ppermute(x, "win", [(i, i ^ bits) for i in range(8)])

    r0, r1, r2, keep0, keep1, send0, send1 = spectra(traces, channel_mask, source_blocks, table)
    p1, p2 = win_swap(r1, PAIRS[1]), win_swap(r2, PAIRS[2])
    part0, part1 = keep0 + chan_swap(send0, 1), keep1 + chan_swap(send1, 1)
    pick, pick_sent = pick_rows()
    for one, other in ((8, 2), (2, 8), (6, 6)):
        part0, part1 = part0 + chan_swap(part0, one), part1 + chan_swap(part1, other)
        if other == 8:
            part0, part1, r0, pick, pick_sent = lax.optimization_barrier(
                (part0, part1, r0, pick, pick_sent)
            )
            p0 = win_swap(r0, PAIRS[0])
    part0, part1, p1, p2 = lax.optimization_barrier((part0, part1, p1, p2))
    part = jnp.concatenate([part0, part1])
    to_y, to_a, to_b = narrow([part0, part1])
    from_a, from_b = win_swap(to_a, PAIRS[1]), win_swap(to_b, PAIRS[2])
    from_y = win_swap(to_y, PAIRS[0])
    s0, s1, s2 = correlate_own(pick, (part, chan_swap(part, 1)), (r0, r1, r2))
    from_a, from_b, s0, s1, s2 = lax.optimization_barrier((from_a, from_b, s0, s1, s2))
    senders = [x for half in (from_a, from_b) for x in (half, chan_swap(half, 1))]
    y, xa, xb, k1, k13, k10, k2, k21, k20 = correlate(
        (1, 2), PARTS_12, (0, 1), pick_sent, lags, senders, (p1, p2), (s1, s2)
    )
    from_y, p0, y, xa, xb = lax.optimization_barrier((from_y, p0, y, xa, xb))
    y1, xa1, xb1 = win_swap(y, (1, 0)), win_swap(xa, (0, 1)), win_swap(xb, (0, 3))
    senders = [from_y, chan_swap(from_y, 1)]
    ua, ub, g0, g1, g3 = correlate((0,), PARTS_0, (0, 1), pick_sent, lags, senders, (p0,), (s0,))
    ua, ub = win_swap(ua, (0, 1)), win_swap(ub, (0, 3))
    ma, mb = merge(merge_once_kernel, [k13, k21, y1], [1, 1])
    xa1, xb1, ma, mb = lax.optimization_barrier((xa1, xb1, ma, mb))
    (y2,) = merge(merge_thirds_kernel, [k10, k20, xa1, xb1], [6])
    y2 = win_swap(y2, (1, 0))
    ma, mb = win_swap(ma, (0, 1)), win_swap(mb, (0, 3))
    xa2, xb2 = merge(merge_ring_kernel, [g1, g3, ua, ub], [4, 4])
    xa2, xb2 = win_swap(xa2, (0, 1)), win_swap(xb2, (0, 3))
    return finish([k1, k2, y1, xa1, xb1, g0, y2, xa2, xb2, ma, mb], channels)


def solution(mesh):
    in_specs = (P("win", None, "chan", None), P("chan"), P())
    out_specs = P("win", None, "chan", None)
    return jax.shard_map(
        on_device, mesh=mesh, in_specs=in_specs, out_specs=out_specs, check_vma=False
    )
```
